128 devices in a mesh: dp: 8 (over z_hi, y), segment: 2 (over core), tile: 8 (over z_lo, x).
Axes of the slice: x: 4, y: 4, z: 4 (z_hi: 2, z_lo: 2; z = z_hi * 2 + z_lo), core: 2. Of those that a mesh axis runs over, the one named last changes fastest.
Arguments:
- coarse: bfloat16 [8, 128, 1024, 128], P('dp', ('segment', 'tile')), may hold values from -6 to 6
- static_fields: bfloat16 [128, 1024, 128], P(('segment', 'tile')), may hold values from -6 to 6
- target: bfloat16 [8, 128, 1024, 128], P('dp', ('segment', 'tile')), may hold values from -6 to 6
- noise: bfloat16 [8, 128, 1024, 128], P('dp', ('segment', 'tile')), may hold values from -6 to 6
- sigma: float32 [8], P('dp'), may hold values from 0.2 to 5
- proj_in: bfloat16 [2, 256, 128], replicated, may hold values from -0.375 to 0.375
- kern_one: bfloat16 [2, 1152, 128], replicated, may hold values from -0.1875 to 0.1875
- kern_two: bfloat16 [2, 1152, 128], replicated, may hold values from -0.1875 to 0.1875
- proj_out: bfloat16 [2, 128, 128], replicated, may hold values from -0.5 to 0.5
Outputs:
- grad_proj_in: float32 [256, 128], replicated
- grad_kern_one: float32 [1152, 128], replicated
- grad_kern_two: float32 [1152, 128], replicated
- grad_proj_out: float32 [128, 128], replicated
The draws below stay inside these ranges and needn't reach their ends.
All inputs are finite; a program needn't handle non-finite values.
Results may differ from the reference program's by a relative error of at most 0.0017.
Values may be sent and summed in bfloat16 or wider, within the bound.
No kernel may reach another device: no remote copies, remote signals or barrier semaphores. Data moves between devices by JAX's collectives and lax.ppermute only.
A program may use at most 128 MiB of HBM per device.

```python
import math
import jax
import jax.numpy as jnp
from jax import lax

C = 128
GW = 1024
BATCH = 8
H = 128


def level_of(rng, shape, shards, smallest, top_value):
    def one(dim, blocks):
        draws = jax.random.uniform(jax.random.fold_in(jax.random.fold_in(rng, 6), dim), (blocks,), jnp.float32, smallest / len(shards), top_value / len(shards))
        return jnp.repeat(jnp.exp(draws), shape[dim] // blocks).reshape((-1,) + (1,) * (len(shape) - dim - 1))

    factor_of = one(*shards[0])
    for cut in shards[1:]:
        factor_of = factor_of * one(*cut)
    return factor_of


def centred(own_key, dims, spread, reach, pieces=(), kind=jnp.bfloat16):
    values = jax.random.normal(own_key, dims, jnp.float32) * spread
    if len(pieces) > 0:
        values = level_of(own_key, dims, pieces, -0.22, 0.18) * values
    return jnp.clip(values, min=-reach, max=reach).astype(kind)


def setup_inputs(seed: int = 0) -> dict:
    splits = jax.random.split(jax.random.key(seed), 10)
    return {
        "coarse": centred(splits[0], (BATCH, H, GW, C), 1.0, 6.0, ((0, 8), (1, 16))),
        "static_fields": centred(splits[1], (H, GW, C), 1.0, 6.0, ((0, 16),)),
        "target": centred(splits[2], (BATCH, H, GW, C), 1.0, 6.0, ((0, 8), (1, 16))),
        "noise": centred(splits[3], (BATCH, H, GW, C), 1.0, 6.0, ((0, 8), (1, 16))),
        "sigma": jnp.clip(jnp.exp(math.log(5.0) - 3.218876 * jax.random.uniform(splits[4], (BATCH,), jnp.float32) ** level_of(splits[4], (BATCH,), ((0, 8),), -0.2, 0.2)), 0.2, 5.0),
        "proj_in": centred(splits[5], (2, 2 * C, C), (2 * C) ** -0.5, 0.375),
        "kern_one": centred(splits[6], (2, 9 * C, C), (9 * C) ** -0.5, 0.1875),
        "kern_two": centred(splits[7], (2, 9 * C, C), (9 * C) ** -0.5, 0.1875),
        "proj_out": centred(splits[8], (2, C, C), C ** -0.5, 0.5),
    }


def conv(padded, kern):
    chan = padded.shape[-1]
    rows = padded.shape[1] - 2
    cols = padded.shape[2]
    wide = jnp.pad(padded, ((0, 0), (0, 0), (1, 1), (0, 0))).astype(jnp.float32)
    total = jnp.zeros((padded.shape[0], rows, cols, kern.shape[1]), jnp.float32)
    for row_tap in range(3):
        band = wide[:, row_tap:row_tap + rows]
        stacked = jnp.concatenate([band[:, :, col_tap:col_tap + cols] for col_tap in range(3)], axis=-1)
        block = kern[row_tap * 3 * chan:(row_tap + 1) * 3 * chan].astype(jnp.float32)
        total = total + jnp.einsum('brwk,kc->brwc', stacked, block)
    return total

def kernel_grad(padded, grad):
    rows = padded.shape[1] - 2
    cols = padded.shape[2]
    wide = jnp.pad(padded, ((0, 0), (0, 0), (1, 1), (0, 0))).astype(jnp.float32)
    blocks = []
    for row_tap in range(3):
        band = wide[:, row_tap:row_tap + rows]
        stacked = jnp.concatenate([band[:, :, col_tap:col_tap + cols] for col_tap in range(3)], axis=-1)
        blocks.append(jnp.einsum('brwk,brwc->kc', stacked, grad.astype(jnp.float32)))
    return jnp.concatenate(blocks, axis=0)

def flipped(kern):
    chan = kern.shape[1]
    return kern.reshape(3, 3, chan, chan)[::-1, ::-1].transpose(0, 1, 3, 2).reshape(9 * chan, chan)

def pad_rows(field):
    return jnp.pad(field, ((0, 0), (1, 1), (0, 0), (0, 0)))

def section(proj_in, kern_one, kern_two, proj_out, first, second):
    joined = jnp.concatenate([first, second], axis=-1)
    h_zero = jnp.einsum('brwk,kc->brwc', joined.astype(jnp.float32), proj_in.astype(jnp.float32)).astype(jnp.bfloat16)
    h_pad = pad_rows(h_zero)
    g_one = conv(h_pad, kern_one)
    u_pad = pad_rows(jax.nn.silu(g_one).astype(jnp.bfloat16))
    hidden = (h_zero.astype(jnp.float32) + conv(u_pad, kern_two)).astype(jnp.bfloat16)
    result = jnp.einsum('brwk,kc->brwc', hidden.astype(jnp.float32), proj_out.astype(jnp.float32))
    return (joined, h_pad, g_one, u_pad, hidden, result)

def reference(coarse, static_fields, target, noise, sigma, proj_in, kern_one, kern_two, proj_out):
    cells = BATCH * H * GW

    def one_sample(index):
        low = lax.dynamic_index_in_dim(coarse, index, 0, True)
        truth = lax.dynamic_index_in_dim(target, index, 0, True)
        unit = lax.dynamic_index_in_dim(noise, index, 0, True)
        level = lax.dynamic_index_in_dim(sigma, index, 0, False)
        *_, first_out = section(proj_in[0], kern_one[0], kern_two[0], proj_out[0], low, static_fields[None])
        mean = first_out.astype(jnp.bfloat16)
        residual = truth.astype(jnp.float32) - mean.astype(jnp.float32)
        noisy = residual + level * unit.astype(jnp.float32)
        total_var = level * level + 1.0
        c_in = 1.0 / jnp.sqrt(total_var)
        c_skip = 1.0 / total_var
        c_out = level / jnp.sqrt(total_var)
        weight = total_var / (level * level)
        scaled = (c_in * noisy).astype(jnp.bfloat16)
        joined, h_pad, g_one, u_pad, hidden, result = section(proj_in[1], kern_one[1], kern_two[1], proj_out[1], scaled, low)
        error = c_skip * noisy + c_out * result - residual
        d_out = (2.0 * weight * c_out / cells * error).astype(jnp.bfloat16)
        g_out = jnp.einsum('brwk,brwc->kc', hidden.astype(jnp.float32), d_out.astype(jnp.float32))
        d_hidden = jnp.einsum('brwc,kc->brwk', d_out.astype(jnp.float32), proj_out[1].astype(jnp.float32)).astype(jnp.bfloat16)
        g_two = kernel_grad(u_pad, d_hidden)
        d_u = conv(pad_rows(d_hidden), flipped(kern_two[1]))
        sig = jax.nn.sigmoid(g_one)
        d_g = (d_u * sig * (1.0 + g_one * (1.0 - sig))).astype(jnp.bfloat16)
        g_one_k = kernel_grad(h_pad, d_g)
        d_zero = (d_hidden.astype(jnp.float32) + conv(pad_rows(d_g), flipped(kern_one[1]))).astype(jnp.bfloat16)
        g_in = jnp.einsum('brwk,brwc->kc', joined.astype(jnp.float32), d_zero.astype(jnp.float32))
        return (g_in, g_one_k, g_two, g_out)
    parts = lax.map(one_sample, jnp.arange(BATCH, dtype=jnp.int32))
    return (lax.optimization_barrier(jnp.sum(parts[0], axis=0)), lax.optimization_barrier(jnp.sum(parts[1], axis=0)), lax.optimization_barrier(jnp.sum(parts[2], axis=0)), lax.optimization_barrier(jnp.sum(parts[3], axis=0)))
```

```python
import jax
import jax.numpy as jnp
from jax import lax
from jax.experimental import pallas as pl
from jax.experimental.pallas import tpu as pltpu
from jax.sharding import PartitionSpec as P

F32 = jnp.float32
BF16 = jnp.bfloat16
C = 128
AXES = ("dp", "segment", "tile")
ROWS = ("segment", "tile")
VMEM = pl.BlockSpec(memory_space=pltpu.VMEM)
SMEM = pl.BlockSpec(memory_space=pltpu.SMEM)
MIB = 1 << 20
AT_IN, AT_ONE, AT_TWO, AT_OUT, FLAT = 0, 256, 1408, 2560, 2816


def dot(a, b):
    return jnp.dot(a, b, preferred_element_type=F32)


def dot_t(a, b):
    return lax.dot_general(a, b, (((0,), (0,)), ((), ())), preferred_element_type=F32)


def zero_pads(tmp):
    width = tmp.shape[1] - 16
    for i in range(tmp.shape[0]):
        tmp[i, 0:8, :] = jnp.zeros((8, C), F32)
        tmp[i, width + 8 : width + 16, :] = jnp.zeros((8, C), F32)


def put(sh, i, tmp, value):
    width = tmp.shape[1] - 16
    row = tmp.at[i % tmp.shape[0]]
    wide = value.astype(F32)
    row[8 : width + 8, :] = wide
    sh[i, :, 0:C] = row[7 : width + 7, :].astype(BF16)
    sh[i, :, C : 2 * C] = value.astype(BF16)
    sh[i, :, 2 * C : 3 * C] = row[9 : width + 9, :].astype(BF16)


def expand(wx, kern):
    tap = 3 * C
    blank = jnp.zeros((tap, C), BF16)
    for j in range(4):
        rows = slice(j * tap, (j + 1) * tap)
        wx[rows, 0:C] = kern[j * tap : (j + 1) * tap, :] if j < 3 else blank
        wx[rows, C : 2 * C] = kern[(j - 1) * tap : j * tap, :] if j > 0 else blank


def diagonal(ox, proj):
    blank = jnp.zeros((C, C), BF16)
    ox[0:C, 0:C] = proj
    ox[C : 2 * C, C : 2 * C] = proj
    ox[0:C, C : 2 * C] = blank
    ox[C : 2 * C, 0:C] = blank


def conv_pair(sh, i, wx):
    return dot(jnp.concatenate([sh[i + j] for j in range(4)], axis=1), wx[...])


def call(body, outs, ins, scratch, limit):
    specs = [SMEM if i.ndim == 1 else VMEM for i in ins]
    return pl.pallas_call(
        body,
        out_shape=[jax.ShapeDtypeStruct(*o) for o in outs],
        in_specs=specs,
        out_specs=[VMEM] * len(outs),
        scratch_shapes=scratch,
        compiler_params=pltpu.CompilerParams(vmem_limit_bytes=limit * MIB),
    )(*ins)


def silu(g):
    s = 0.5 * jnp.tanh(0.5 * g) + 0.5
    return g * s, s


def edge_entry(coarse, statics, proj):
    width = coarse.shape[2]

    def body(c_ref, s_ref, p_ref, o_ref):
        for r in range(2):
            both = jnp.concatenate([c_ref[0, r], s_ref[r]], axis=1)
            o_ref[0, r] = dot(both, p_ref[...]).astype(BF16)

    out = pl.pallas_call(
        body,
        grid=(2,),
        out_shape=jax.ShapeDtypeStruct((2, 2, width, C), BF16),
        in_specs=[
            pl.BlockSpec((1, 2, width, C), lambda i: (0, 3 * i, 0, 0)),
            pl.BlockSpec((2, width, C), lambda i: (3 * i, 0, 0)),
            pl.BlockSpec((2 * C, C), lambda i: (0, 0)),
        ],
        out_specs=pl.BlockSpec((1, 2, width, C), lambda i: (i, 0, 0, 0)),
        compiler_params=pltpu.CompilerParams(vmem_limit_bytes=12 * MIB),
    )(coarse, statics, proj)
    return out


def finish_mean(h, pair, at, r, ox, target, noise, coarse, level, c_in, p_ref, mean, a, h_zero):
    both = dot(h, ox[...])
    for k in range(2):
        m = both[:, k * C : (k + 1) * C].astype(BF16)
        mean[at + k] = m
        residual = target[0, r + k].astype(F32) - m.astype(F32)
        noisy = residual + level * noise[0, r + k].astype(F32)
        scaled = (c_in * noisy).astype(BF16)
        a[at + k] = scaled
        joined = jnp.concatenate([scaled, coarse[0, r + k]], axis=1)
        h_zero[at + k] = dot(joined, p_ref[...]).astype(BF16)


def add_pair(first, second, conv):
    return jnp.concatenate(
        [
            (first.astype(F32) + conv[:, 0:C]).astype(BF16),
            (second.astype(F32) + conv[:, C : 2 * C]).astype(BF16),
        ],
        axis=1,
    )


def mean_inside(edges, coarse, statics, target, noise, scalars, p_reg, k_one, k_two, o_reg, p_dif):
    width = coarse.shape[2]

    def body(e_ref, c_ref, s_ref, t_ref, n_ref, sc, p_ref, k1, k2, o_ref, pd_ref,
             u_out, mean, a, h_zero, hs, us, tmp, w1, w2, ox):
        zero_pads(tmp)
        expand(w1, k1)
        expand(w2, k2)
        diagonal(ox, o_ref[...])
        for r in range(8):
            if r in (0, 1, 6, 7):
                value = e_ref[r // 6, r % 2]
            else:
                both = jnp.concatenate([c_ref[0, r], s_ref[r]], axis=1)
                value = dot(both, p_ref[...]).astype(BF16)
            put(hs, r, tmp, value)
        for r in (1, 3, 5):
            g = conv_pair(hs, r - 1, w1)
            for k in range(2):
                u, _ = silu(g[:, k * C : (k + 1) * C])
                u = u.astype(BF16)
                put(us, r + k - 1, tmp, u)
                if r != 3:
                    u_out[(r // 5) * 2 + k] = u
        for r in (2, 4):
            conv = conv_pair(us, r - 2, w2)
            h = add_pair(hs[r, :, C : 2 * C], hs[r + 1, :, C : 2 * C], conv)
            finish_mean(h, conv, r - 2, r, ox, t_ref, n_ref, c_ref, sc[0], sc[1], pd_ref,
                        mean, a, h_zero)

    four = ((4, width, C), BF16)
    return call(
        body,
        [four] * 4,
        [edges, coarse, statics, target, noise, scalars, p_reg, k_one, k_two, o_reg, p_dif],
        [
            pltpu.VMEM((8, width, 3 * C), BF16),
            pltpu.VMEM((6, width, 3 * C), BF16),
            pltpu.VMEM((4, width + 16, C), F32),
            pltpu.VMEM((12 * C, 2 * C), BF16),
            pltpu.VMEM((12 * C, 2 * C), BF16),
            pltpu.VMEM((2 * C, 2 * C), BF16),
        ],
        40,
    )


def mean_edge(low, high, edges, u_in, coarse, target, noise, scalars, k_one, k_two, o_reg, p_dif):
    width = coarse.shape[2]

    def body(lo, hi, e_ref, ui, c_ref, t_ref, n_ref, sc, k1, k2, o_ref, pd_ref,
             mean, a, h_zero, hs, us, tmp, w1, w2, ox):
        zero_pads(tmp)
        expand(w1, k1)
        expand(w2, k2)
        diagonal(ox, o_ref[...])
        for side in range(2):
            halo = (lo, hi)[side]
            keep = sc[6 + side]
            for k in range(2):
                masked = halo[k].astype(F32) * keep
                put(hs, 4 * side + (k if side == 0 else 2 + k), tmp, masked)
                put(hs, 4 * side + (2 + k if side == 0 else k), tmp, e_ref[side, k])
            g = conv_pair(hs, 4 * side, w1)
            for k in range(2):
                u, _ = silu(g[:, k * C : (k + 1) * C])
                if k == side:
                    u = u * keep
                put(us, 4 * side + (k if side == 0 else 2 + k), tmp, u.astype(BF16))
                put(us, 4 * side + (2 + k if side == 0 else k), tmp, ui[2 * side + k])
            conv = conv_pair(us, 4 * side, w2)
            h = add_pair(e_ref[side, 0], e_ref[side, 1], conv)
            finish_mean(h, conv, 0, 6 * side, ox, t_ref, n_ref, c_ref, sc[0], sc[1], pd_ref,
                        mean.at[side], a.at[side], h_zero.at[side])

    edge = ((2, 2, width, C), BF16)
    return call(
        body,
        [edge] * 3,
        [low, high, edges, u_in, coarse, target, noise, scalars, k_one, k_two, o_reg, p_dif],
        [
            pltpu.VMEM((8, width, 3 * C), BF16),
            pltpu.VMEM((8, width, 3 * C), BF16),
            pltpu.VMEM((4, width + 16, C), F32),
            pltpu.VMEM((12 * C, 2 * C), BF16),
            pltpu.VMEM((12 * C, 2 * C), BF16),
            pltpu.VMEM((2 * C, 2 * C), BF16),
        ],
        40,
    )


def finish_forward(h, at, r, ox, oy, target, noise, mean, sc, hidden, d_out, d_hidden):
    both = dot(h, ox[...])
    grads = []
    for k in range(2):
        hidden[at + k] = h[:, k * C : (k + 1) * C]
        residual = target[0, r + k].astype(F32) - mean[at + k].astype(F32)
        noisy = residual + sc[0] * noise[0, r + k].astype(F32)
        error = sc[2] * noisy + sc[3] * both[:, k * C : (k + 1) * C] - residual
        grad = (sc[4] * error).astype(BF16)
        d_out[at + k] = grad
        grads.append(grad)
    back = dot(jnp.concatenate(grads, axis=1), oy[...]).astype(BF16)
    for k in range(2):
        d_hidden[at + k] = back[:, k * C : (k + 1) * C]


def forward_inside(edges, middle, mean, target, noise, scalars, k_one, k_two, o_dif, o_back):
    width = target.shape[2]

    def body(e_ref, m_ref, mean_ref, t_ref, n_ref, sc, k1, k2, o_ref, ob_ref,
             u_out, slope, hidden, d_out, d_hidden, hs, us, tmp, w1, w2, ox, oy):
        zero_pads(tmp)
        expand(w1, k1)
        expand(w2, k2)
        diagonal(ox, o_ref[...])
        diagonal(oy, ob_ref[...])
        for r in range(8):
            put(hs, r, tmp, e_ref[r // 6, r % 2] if r in (0, 1, 6, 7) else m_ref[r - 2])
        for r in (1, 3, 5):
            g = conv_pair(hs, r - 1, w1)
            for k in range(2):
                u, s = silu(g[:, k * C : (k + 1) * C])
                slope[r + k - 1] = (s + u * (1.0 - s)).astype(BF16)
                u = u.astype(BF16)
                u_out[r + k - 1] = u
                put(us, r + k - 1, tmp, u)
        for r in (2, 4):
            conv = conv_pair(us, r - 2, w2)
            h = add_pair(m_ref[r - 2], m_ref[r - 1], conv)
            finish_forward(h, r - 2, r, ox, oy, t_ref, n_ref, mean_ref, sc,
                           hidden, d_out, d_hidden)

    four = ((4, width, C), BF16)
    six = ((6, width, C), BF16)
    return call(
        body,
        [six, six, four, four, four],
        [edges, middle, mean, target, noise, scalars, k_one, k_two, o_dif, o_back],
        [
            pltpu.VMEM((8, width, 3 * C), BF16),
            pltpu.VMEM((6, width, 3 * C), BF16),
            pltpu.VMEM((4, width + 16, C), F32),
            pltpu.VMEM((12 * C, 2 * C), BF16),
            pltpu.VMEM((12 * C, 2 * C), BF16),
            pltpu.VMEM((2 * C, 2 * C), BF16),
            pltpu.VMEM((2 * C, 2 * C), BF16),
        ],
        40,
    )


def forward_edge(low, high, edges, u_in, mean, target, noise, scalars, k_one, k_two, o_dif, o_back):
    width = target.shape[2]

    def body(lo, hi, e_ref, ui, mean_ref, t_ref, n_ref, sc, k1, k2, o_ref, ob_ref,
             u_out, slope, hidden, d_out, d_hidden, hs, us, tmp, w1, w2, ox, oy):
        zero_pads(tmp)
        expand(w1, k1)
        expand(w2, k2)
        diagonal(ox, o_ref[...])
        diagonal(oy, ob_ref[...])
        for side in range(2):
            halo = (lo, hi)[side]
            keep = sc[6 + side]
            for k in range(2):
                masked = halo[k].astype(F32) * keep
                put(hs, 4 * side + (k if side == 0 else 2 + k), tmp, masked)
                put(hs, 4 * side + (2 + k if side == 0 else k), tmp, e_ref[side, k])
            g = conv_pair(hs, 4 * side, w1)
            for k in range(2):
                u, s = silu(g[:, k * C : (k + 1) * C])
                rate = s + u * (1.0 - s)
                if k == side:
                    u = u * keep
                    rate = rate * keep
                slope[side, k] = rate.astype(BF16)
                u = u.astype(BF16)
                u_out[side, k] = u
                put(us, 4 * side + (k if side == 0 else 2 + k), tmp, u)
                put(us, 4 * side + (2 + k if side == 0 else k), tmp, ui[4 * side + k])
            conv = conv_pair(us, 4 * side, w2)
            h = add_pair(e_ref[side, 0], e_ref[side, 1], conv)
            finish_forward(h, 0, 6 * side, ox, oy, t_ref, n_ref, mean_ref.at[side], sc,
                           hidden.at[side], d_out.at[side], d_hidden.at[side])

    edge = ((2, 2, width, C), BF16)
    return call(
        body,
        [edge] * 5,
        [low, high, edges, u_in, mean, target, noise, scalars, k_one, k_two, o_dif, o_back],
        [
            pltpu.VMEM((8, width, 3 * C), BF16),
            pltpu.VMEM((8, width, 3 * C), BF16),
            pltpu.VMEM((4, width + 16, C), F32),
            pltpu.VMEM((12 * C, 2 * C), BF16),
            pltpu.VMEM((12 * C, 2 * C), BF16),
            pltpu.VMEM((2 * C, 2 * C), BF16),
            pltpu.VMEM((2 * C, 2 * C), BF16),
        ],
        40,
    )


def taps(sh, i):
    return jnp.concatenate([sh[i + j] for j in range(3)], axis=1)


def backward_inside(u_edge, u_mid, slope, h_edge, h_mid, hid_edge, hid_mid, do_edge, do_mid,
                    dh_edge, dh_mid, a_mid, coarse, k_one_t, k_two_t):
    width = coarse.shape[2]

    def body(ue, um, sl, he, hm, hide, hidm, doe, dom, dhe, dhm, am, c_ref, k1, k2,
             g_two, g_out, g_one, g_in, d_g, rows, ds, gs, tmp, w1, w2):
        zero_pads(tmp)
        expand(w1, k1)
        expand(w2, k2)

        def pick(edge, mid, r):
            return edge[r // 6, r % 2] if r in (0, 1, 6, 7) else mid[r - 2]

        for r in range(-1, 9):
            if r < 1:
                value = ue[0, r + 1]
            elif r > 6:
                value = ue[1, r - 7]
            else:
                value = um[r - 1]
            put(rows, r + 1, tmp, value)
        total = None
        for r in range(8):
            part = dot_t(pick(dhe, dhm, r), taps(rows, r))
            total = part if total is None else total + part
        g_two[...] = total
        total = None
        for r in range(8):
            part = dot_t(pick(hide, hidm, r), pick(doe, dom, r))
            total = part if total is None else total + part
        g_out[...] = total
        for r in range(8):
            put(ds, r, tmp, pick(dhe, dhm, r))
        for r in (1, 3, 5):
            d_u = conv_pair(ds, r - 1, w2)
            for k in range(2):
                grad = (d_u[:, k * C : (k + 1) * C] * sl[r + k - 1].astype(F32)).astype(BF16)
                put(gs, r + k - 1, tmp, grad)
                if r != 3:
                    d_g[(r // 5) * 2 + k] = grad
        for r in range(8):
            put(rows, r, tmp, pick(he, hm, r))
        total = None
        for r in range(1, 7):
            part = dot_t(gs[r - 1, :, C : 2 * C], taps(rows, r - 1))
            total = part if total is None else total + part
        g_one[...] = total
        total = None
        for r in (2, 4):
            conv = conv_pair(gs, r - 2, w1)
            d_zero = add_pair(dhm[r - 2], dhm[r - 1], conv)
            for k in range(2):
                joined = jnp.concatenate([am[r + k - 2], c_ref[0, r + k]], axis=1)
                part = dot_t(d_zero[:, k * C : (k + 1) * C], joined)
                total = part if total is None else total + part
        g_in[...] = total

    return call(
        body,
        [
            ((C, 9 * C), F32),
            ((C, C), F32),
            ((C, 9 * C), F32),
            ((C, 2 * C), F32),
            ((4, width, C), BF16),
        ],
        [u_edge, u_mid, slope, h_edge, h_mid, hid_edge, hid_mid, do_edge, do_mid,
         dh_edge, dh_mid, a_mid, coarse, k_one_t, k_two_t],
        [
            pltpu.VMEM((10, width, 3 * C), BF16),
            pltpu.VMEM((8, width, 3 * C), BF16),
            pltpu.VMEM((6, width, 3 * C), BF16),
            pltpu.VMEM((4, width + 16, C), F32),
            pltpu.VMEM((12 * C, 2 * C), BF16),
            pltpu.VMEM((12 * C, 2 * C), BF16),
        ],
        46,
    )


def backward_edge(low, high, dh_edge, d_g, slope, h_low, h_high, h_edge, h_mid, a_edge, coarse,
                  g_two, g_out, g_one, g_in, scalars, place, k_one_t, k_two_t):
    width = coarse.shape[2]

    def body(lo, hi, dhe, dgi, sl, hlo, hhi, he, hm, ae, c_ref, g2, go, g1, gi, sc, at, k1, k2,
             keep_out, send_out, ds, gs, hs, tmp, w1, w2, flat):
        zero_pads(tmp)
        expand(w1, k1)
        expand(w2, k2)
        sum_one = g1[...]
        sum_in = gi[...]
        for side in range(2):
            halo = (lo, hi)[side]
            h_halo = (hlo, hhi)[side]
            keep = sc[6 + side]
            base = 4 * side
            for k in range(2):
                masked = halo[k].astype(F32) * keep
                put(ds, base + (k if side == 0 else 2 + k), tmp, masked)
                put(ds, base + (2 + k if side == 0 else k), tmp, dhe[side, k])
            d_u = conv_pair(ds, base, w2)
            for k in range(2):
                grad = (d_u[:, k * C : (k + 1) * C] * sl[side, k].astype(F32)).astype(BF16)
                put(gs, base + (k if side == 0 else 2 + k), tmp, grad)
                put(gs, base + (2 + k if side == 0 else k), tmp, dgi[2 * side + k])
            if side == 0:
                near = [h_halo[1].astype(F32) * keep, he[0, 0], he[0, 1]]
            else:
                near = [he[1, 0], he[1, 1], h_halo[0].astype(F32) * keep]
            for k in range(3):
                put(hs, base + k, tmp, near[k])
            own = gs[base + (1 if side == 0 else 2), :, C : 2 * C]
            sum_one = sum_one + dot_t(own, taps(hs, base))
            conv = conv_pair(gs, base, w1)
            d_zero = add_pair(dhe[side, 0], dhe[side, 1], conv)
            for k in range(2):
                joined = jnp.concatenate([ae[side, k], c_ref[0, 6 * side + k]], axis=1)
                sum_in = sum_in + dot_t(d_zero[:, k * C : (k + 1) * C], joined)
        for k in range(9):
            flat[AT_ONE + k * C : AT_ONE + (k + 1) * C, :] = sum_one[:, k * C : (k + 1) * C].T
            flat[AT_TWO + k * C : AT_TWO + (k + 1) * C, :] = g2[:, k * C : (k + 1) * C].T
        for k in range(2):
            flat[AT_IN + k * C : AT_IN + (k + 1) * C, :] = sum_in[:, k * C : (k + 1) * C].T
        flat[AT_OUT : AT_OUT + C, :] = go[...]
        flat[AT_OUT + C : FLAT, :] = jnp.zeros((FLAT - AT_OUT - C, C), F32)
        half = FLAT // 2
        keep_out[...] = flat[pl.ds(pl.multiple_of(at[0] * half, half), half), :]
        send_out[...] = flat[pl.ds(pl.multiple_of((1 - at[0]) * half, half), half), :]

    half = ((FLAT // 2, C), F32)
    return call(
        body,
        [half, half],
        [low, high, dh_edge, d_g, slope, h_low, h_high, h_edge, h_mid, a_edge, coarse,
         g_two, g_out, g_one, g_in, scalars, place, k_one_t, k_two_t],
        [
            pltpu.VMEM((8, width, 3 * C), BF16),
            pltpu.VMEM((8, width, 3 * C), BF16),
            pltpu.VMEM((8, width, 3 * C), BF16),
            pltpu.VMEM((4, width + 16, C), F32),
            pltpu.VMEM((12 * C, 2 * C), BF16),
            pltpu.VMEM((12 * C, 2 * C), BF16),
            pltpu.VMEM((FLAT, C), F32),
        ],
        46,
    )


def shifted(axis, step):
    pairs = []
    for dp in range(8):
        for segment in range(2):
            for tile in range(8):
                at = {"x": tile % 4, "y": dp % 4, "z": (dp // 4) * 2 + tile // 4, "core": segment}
                to = dict(at)
                to[axis] = (at[axis] + step) % (2 if axis == "core" else 4)
                target = ((to["z"] // 2) * 4 + to["y"]) * 16 + to["core"] * 8
                target += (to["z"] % 2) * 4 + to["x"]
                pairs.append(((dp * 2 + segment) * 8 + tile, target))
    return pairs


def send(value, axis, step):
    return lax.ppermute(value, AXES, shifted(axis, step))


def scalar(value):
    return jnp.asarray(value, jnp.int32).reshape(1)


def split(terms, parts, index):
    rows = terms[0].shape[0] // parts
    count = len(terms)

    def body(*refs):
        at = refs[0]
        for j in range(parts):
            start = pl.multiple_of(lax.rem(at[0] + j, parts) * rows, 8)
            total = refs[1][pl.ds(start, rows), :]
            for term in refs[2 : 1 + count]:
                total = total + term[pl.ds(start, rows), :]
            refs[1 + count + j][...] = total

    return call(body, [((rows, C), F32)] * parts, [scalar(index), *terms], [], 8)


def join(chunks, index):
    rows = chunks[0].shape[0]
    parts = len(chunks)

    def body(*refs):
        at = refs[0]
        for j in range(parts):
            start = pl.multiple_of(lax.rem(at[0] + j, parts) * rows, 8)
            refs[-1][pl.ds(start, rows), :] = refs[1 + j][...]

    return call(body, [((rows * parts, C), F32)], [scalar(index), *chunks], [], 8)[0]


def add(terms):
    def body(*refs):
        total = refs[0][...]
        for term in refs[1:-1]:
            total = total + term[...]
        refs[-1][...] = total

    return call(body, [(terms[0].shape, F32)], terms, [], 8)[0]


def reduce_all(keep, other, core, x, y):
    got = send(other, "core", 1)
    own, *rest = split([keep, got], 4, x)
    got = [send(part, "x", j + 1) for j, part in enumerate(rest)]
    own, *rest = split([own, *got], 4, y)
    got = [send(part, "y", j + 1) for j, part in enumerate(rest)]
    own = add([own, *got])
    own = add([own, *[send(own, "z", j + 1) for j in range(3)]])
    own = join([own, *[send(own, "y", -(j + 1)) for j in range(3)]], y)
    own = join([own, *[send(own, "x", -(j + 1)) for j in range(3)]], x)
    got = send(own, "core", 1)

    def body(at, a_ref, b_ref, g_in, g_one, g_two, g_out):
        half = FLAT // 2
        first = at[0] == 0

        def rows(start, stop):
            if stop <= half:
                span = slice(start, stop)
            else:
                span = slice(start - half, stop - half)
            low = stop <= half
            return jnp.where(first == low, a_ref[span, :], b_ref[span, :])

        g_in[...] = rows(AT_IN, AT_ONE)
        g_one[...] = rows(AT_ONE, AT_TWO)
        g_two[...] = rows(AT_TWO, AT_OUT)
        g_out[...] = rows(AT_OUT, AT_OUT + C)

    return call(
        body,
        [((2 * C, C), F32), ((9 * C, C), F32), ((9 * C, C), F32), ((C, C), F32)],
        [scalar(core), own, got],
        [],
        8,
    )


def flipped(kern):
    return kern.reshape(3, 3, C, C)[::-1, ::-1].transpose(0, 1, 3, 2).reshape(9 * C, C)


def exchange(edges):
    count = lax.axis_size(ROWS)
    down = [(i, (i + 1) % count) for i in range(count)]
    up = [(target, source) for source, target in down]
    return lax.ppermute(edges[1], ROWS, down), lax.ppermute(edges[0], ROWS, up)


def on_device(coarse, static_fields, target, noise, sigma, proj_in, kern_one, kern_two, proj_out):
    segment = lax.axis_index("segment")
    tile = lax.axis_index("tile")
    x = tile % 4
    y = lax.axis_index("dp") % 4
    row = lax.axis_index(ROWS)
    cells = lax.axis_size("dp") * coarse.shape[1] * lax.axis_size(ROWS) * coarse.shape[2]
    level = sigma[0]
    total_var = level * level + 1.0
    c_in = 1.0 / jnp.sqrt(total_var)
    c_out = level / jnp.sqrt(total_var)
    weight = total_var / (level * level)
    scalars = jnp.stack(
        [
            level,
            c_in,
            1.0 / total_var,
            c_out,
            2.0 * weight * c_out / cells,
            jnp.zeros((), F32),
            (row != 0).astype(F32),
            (row != lax.axis_size(ROWS) - 1).astype(F32),
        ]
    )

    reg_edge = edge_entry(coarse, static_fields, proj_in[0])
    low, high = exchange(reg_edge)
    u_in, mean_mid, a_mid, h_mid = mean_inside(
        reg_edge, coarse, static_fields, target, noise, scalars,
        proj_in[0], kern_one[0], kern_two[0], proj_out[0], proj_in[1],
    )
    mean_e, a_edge, h_edge = mean_edge(
        low, high, reg_edge, u_in, coarse, target, noise, scalars,
        kern_one[0], kern_two[0], proj_out[0], proj_in[1],
    )
    h_low, h_high = exchange(h_edge)
    u_mid, slope_mid, hid_mid, do_mid, dh_mid = forward_inside(
        h_edge, h_mid, mean_mid, target, noise, scalars,
        kern_one[1], kern_two[1], proj_out[1], proj_out[1].T,
    )
    u_edge, slope_edge, hid_edge, do_edge, dh_edge = forward_edge(
        h_low, h_high, h_edge, u_mid, mean_e, target, noise, scalars,
        kern_one[1], kern_two[1], proj_out[1], proj_out[1].T,
    )
    dh_low, dh_high = exchange(dh_edge)
    one_t = flipped(kern_one[1])
    two_t = flipped(kern_two[1])
    g_two, g_out, g_one, g_in, d_g = backward_inside(
        u_edge, u_mid, slope_mid, h_edge, h_mid, hid_edge, hid_mid, do_edge, do_mid,
        dh_edge, dh_mid, a_mid, coarse, one_t, two_t,
    )
    keep, other = backward_edge(
        dh_low, dh_high, dh_edge, d_g, slope_edge, h_low, h_high, h_edge, h_mid, a_edge, coarse,
        g_two, g_out, g_one, g_in, scalars, scalar(segment), one_t, two_t,
    )
    return tuple(reduce_all(keep, other, segment, x, y))


def solution(mesh):
    placed = (
        P("dp", ("segment", "tile"), None, None),
        P(("segment", "tile"), None, None),
        P("dp", ("segment", "tile"), None, None),
        P("dp", ("segment", "tile"), None, None),
        P("dp"),
        P(),
        P(),
        P(),
        P(),
    )
    return jax.shard_map(
        on_device, mesh=mesh, in_specs=placed, out_specs=(P(), P(), P(), P()), check_vma=False
    )
```

```python
import jax
import jax.numpy as jnp
from jax import lax
from jax.experimental import pallas as pl
from jax.experimental.pallas import tpu as pltpu
from jax.sharding import PartitionSpec as P

F32 = jnp.float32
BF16 = jnp.bfloat16
C = 128
AXES = ("dp", "segment", "tile")
ROWS = ("segment", "tile")
VMEM = pl.BlockSpec(memory_space=pltpu.VMEM)
SMEM = pl.BlockSpec(memory_space=pltpu.SMEM)
MIB = 1 << 20
LIMIT = 28
ENTRY_LIMIT = 12
SPAN = 1024
AT_IN, AT_ONE, AT_TWO, AT_OUT, FLAT = 0, 256, 1408, 2560, 2816


def dot(a, b):
    return jnp.dot(a, b, preferred_element_type=F32)


def dot_t(a, b):
    return lax.dot_general(a, b, (((0,), (0,)), ((), ())), preferred_element_type=F32)


def clear_rims(*fields):
    for field in fields:
        width = field.shape[1] - 16
        for i in range(field.shape[0]):
            field[i, 0:8, :] = jnp.zeros((8, C), F32)
            field[i, width + 8 : width + 16, :] = jnp.zeros((8, C), F32)


def spans(width, body):
    @pl.loop(0, width // SPAN)
    def _(i):
        body(pl.multiple_of(i * SPAN, SPAN))


def put(field, i, c, value):
    field[i, pl.ds(pl.multiple_of(c + 8, 8), SPAN), :] = value.astype(F32)


def near(field, i, c):
    view = field.at[i, pl.ds(c, SPAN + 16), :]
    return [view[7 + k : 7 + k + SPAN, :].astype(BF16) for k in range(3)]


def expand(wx, kern, transposed=False):
    blank = jnp.zeros((C, C), BF16)
    for row in range(3):
        for col in range(3):
            if transposed:
                at = (8 - 3 * row - col) * C
                tap = kern[1, at : at + C, :].T
            else:
                at = (3 * row + col) * C
                tap = kern[at : at + C, :]
            for k in range(2):
                to = (3 * (row + k) + col) * C
                wx[to : to + C, k * C : (k + 1) * C] = tap
    for col in range(3):
        wx[(9 + col) * C : (10 + col) * C, 0:C] = blank
        wx[col * C : (col + 1) * C, C : 2 * C] = blank


def diagonal(ox, proj):
    blank = jnp.zeros((C, C), BF16)
    ox[0:C, 0:C] = proj
    ox[C : 2 * C, C : 2 * C] = proj
    ox[0:C, C : 2 * C] = blank
    ox[C : 2 * C, 0:C] = blank


def conv_pair(rows, wx):
    return dot(jnp.concatenate(rows[0] + rows[1] + rows[2] + rows[3], axis=1), wx[...])


def kernel_grad(grads, rows):
    wide = [jnp.concatenate(sum(group, []), axis=1) for group in rows]
    return dot_t(jnp.concatenate(grads, axis=0), jnp.concatenate(wide, axis=0))


def windows(rows):
    return [rows[i : i + 3] for i in range(len(rows) - 2)]


def cost(products):
    flops = 2 * 1024 * 12 * C * 2 * C * products
    return pl.CostEstimate(flops=flops, bytes_accessed=2 * MIB, transcendentals=0)


def call(body, outs, ins, scratch, limit, products=0):
    specs = [SMEM if i.ndim == 1 else VMEM for i in ins]
    return pl.pallas_call(
        body,
        out_shape=[jax.ShapeDtypeStruct(*o) for o in outs],
        in_specs=specs,
        out_specs=[VMEM] * len(outs),
        scratch_shapes=scratch,
        compiler_params=pltpu.CompilerParams(vmem_limit_bytes=limit * MIB),
        cost_estimate=cost(products),
    )(*ins)


def silu(g):
    s = 0.5 * jnp.tanh(0.5 * g) + 0.5
    return g * s, s


def half(pair, k):
    return pair[:, k * C : (k + 1) * C]


def pick(top, mid, bottom, r, at):
    if r < 2:
        return top[r, at, :]
    return bottom[r - 6, at, :] if r > 5 else mid[r - 2, at, :]


def add_pair(first, second, conv):
    return jnp.concatenate(
        [
            (first.astype(F32) + half(conv, 0)).astype(BF16),
            (second.astype(F32) + half(conv, 1)).astype(BF16),
        ],
        axis=1,
    )


def padded(count, width):
    return pltpu.VMEM((count, width + 16, C), F32)


WIDE = ((12 * C, 2 * C), BF16)
SQUARE = pltpu.VMEM((2 * C, 2 * C), BF16)


def edge_entry(coarse, statics, proj_in):
    width = coarse.shape[2]

    def body(c_ref, s_ref, p_ref, top, bottom):
        for side, out in ((0, top), (1, bottom)):

            @pl.when(pl.program_id(0) == side)
            def _():
                for r in range(2):
                    both = jnp.concatenate([c_ref[0, r], s_ref[r]], axis=1)
                    out[r] = dot(both, p_ref[0]).astype(BF16)

    two = (2, width, C)
    return pl.pallas_call(
        body,
        grid=(2,),
        out_shape=[jax.ShapeDtypeStruct(two, BF16)] * 2,
        in_specs=[
            pl.BlockSpec((1, *two), lambda i: (0, 3 * i, 0, 0)),
            pl.BlockSpec(two, lambda i: (3 * i, 0, 0)),
            pl.BlockSpec((1, 2 * C, C), lambda i: (0, 0, 0)),
        ],
        out_specs=[pl.BlockSpec(two, lambda i: (0, 0, 0))] * 2,
        compiler_params=pltpu.CompilerParams(vmem_limit_bytes=ENTRY_LIMIT * MIB),
        cost_estimate=cost(1),
    )(coarse, statics, proj_in)


def finish_mean(h, i, r, at, ox, target, noise, coarse, sc, proj_in, mean, a, h_zero):
    both = dot(h, ox[...])
    for k in range(2):
        m = half(both, k).astype(BF16)
        mean[i + k, at, :] = m
        residual = target[0, r + k, at, :].astype(F32) - m.astype(F32)
        noisy = residual + sc[0] * noise[0, r + k, at, :].astype(F32)
        scaled = (sc[1] * noisy).astype(BF16)
        a[i + k, at, :] = scaled
        joined = jnp.concatenate([scaled, coarse[0, r + k, at, :]], axis=1)
        h_zero[i + k, at, :] = dot(joined, proj_in[1]).astype(BF16)


def mean_inside(top, bottom, coarse, statics, target, noise, scalars, proj_in, kern_one,
                kern_two, proj_out):
    width = coarse.shape[2]

    def body(top_ref, bot_ref, c_ref, s_ref, t_ref, n_ref, sc, p_ref, k1, k2, o_ref,
             u_out, mean, a, h_zero, w1, w2, hs, us, ox):
        clear_rims(hs, us)
        expand(w1, k1.at[0])
        expand(w2, k2.at[0])
        diagonal(ox, o_ref[0])

        def entry(c):
            at = pl.ds(c, SPAN)
            for r in range(8):
                if r in (2, 3, 4, 5):
                    both = jnp.concatenate([c_ref[0, r, at, :], s_ref[r, at, :]], axis=1)
                    put(hs, r, c, dot(both, p_ref[0]).astype(BF16))
                else:
                    put(hs, r, c, (top_ref, bot_ref)[r // 6][r % 2, at, :])

        def first(c):
            at = pl.ds(c, SPAN)
            rows = [near(hs, r, c) for r in range(8)]
            for r in (1, 3, 5):
                g = conv_pair(rows[r - 1 : r + 3], w1)
                for k in range(2):
                    u = silu(half(g, k))[0].astype(BF16)
                    put(us, r + k - 1, c, u)
                    if r != 3:
                        u_out[(r // 5) * 2 + k, at, :] = u

        def second(c):
            at = pl.ds(c, SPAN)
            rows = [near(us, r, c) for r in range(6)]
            for r in (2, 4):
                conv = conv_pair(rows[r - 2 : r + 2], w2)
                own = [hs[r + k, pl.ds(pl.multiple_of(c + 8, 8), SPAN), :] for k in range(2)]
                h = add_pair(*own, conv)
                finish_mean(h, r - 2, r, at, ox, t_ref, n_ref, c_ref, sc, p_ref, mean, a, h_zero)

        spans(width, entry)
        spans(width, first)
        spans(width, second)

    four = ((4, width, C), BF16)
    return call(
        body,
        [four, four, four, four, WIDE, WIDE],
        [top, bottom, coarse, statics, target, noise, scalars, proj_in, kern_one, kern_two,
         proj_out],
        [padded(8, width), padded(6, width), SQUARE],
        LIMIT,
        6,
    )


def ordered(side, own, out):
    return own + out if side else out + own


def mean_edge(low, high, top, bottom, u_in, coarse, target, noise, scalars, proj_in, w_one, w_two,
              proj_out):
    width = coarse.shape[2]

    def body(lo, hi, top_ref, bot_ref, ui, c_ref, t_ref, n_ref, sc, p_ref, w1, w2, o_ref,
             mean_t, mean_b, a_t, a_b, hz_t, hz_b, hs, us, ox):
        clear_rims(hs, us)
        diagonal(ox, o_ref[0])
        edges = (top_ref, bot_ref)

        def entry(c):
            at = pl.ds(c, SPAN)
            for side in range(2):
                for k in range(2):
                    outer = (lo, hi)[side][k, at, :].astype(F32) * sc[6 + side]
                    put(hs, 6 * side + k, c, outer)
                    put(hs, 2 + 2 * side + k, c, edges[side][k, at, :])
                    put(us, 2 + 2 * side + k, c, ui[2 * side + k, at, :])

        def first(c):
            for side in range(2):
                rows = [near(hs, 4 * side + j, c) for j in range(4)]
                g = conv_pair(rows, w1)
                for k in range(2):
                    u, _ = silu(half(g, k))
                    if k == side:
                        u = u * sc[6 + side]
                    put(us, 6 * side + k, c, u.astype(BF16))

        def second(c):
            at = pl.ds(c, SPAN)
            for side in range(2):
                conv = conv_pair([near(us, 4 * side + j, c) for j in range(4)], w2)
                h = add_pair(edges[side][0, at, :], edges[side][1, at, :], conv)
                finish_mean(h, 0, 6 * side, at, ox, t_ref, n_ref, c_ref, sc, p_ref,
                            (mean_t, mean_b)[side], (a_t, a_b)[side], (hz_t, hz_b)[side])

        spans(width, entry)
        spans(width, first)
        spans(width, second)

    two = ((2, width, C), BF16)
    return call(
        body,
        [two] * 6,
        [low, high, top, bottom, u_in, coarse, target, noise, scalars, proj_in, w_one, w_two,
         proj_out],
        [padded(8, width), padded(8, width), SQUARE],
        LIMIT,
        5,
    )


def finish_forward(h, i, r, at, ox, oy, target, noise, mean, sc, hidden, d_out, d_hidden):
    both = dot(h, ox[...])
    grads = []
    for k in range(2):
        hidden[i + k, at, :] = half(h, k)
        residual = target[0, r + k, at, :].astype(F32) - mean[i + k, at, :].astype(F32)
        noisy = residual + sc[0] * noise[0, r + k, at, :].astype(F32)
        error = sc[2] * noisy + sc[3] * half(both, k) - residual
        grad = (sc[4] * error).astype(BF16)
        d_out[i + k, at, :] = grad
        grads.append(grad)
    back = dot(jnp.concatenate(grads, axis=1), oy[...]).astype(BF16)
    for k in range(2):
        d_hidden[i + k, at, :] = half(back, k)
    return grads, [half(back, 0), half(back, 1)]


def forward_inside(top, middle, bottom, mean, target, noise, scalars, kern_one, kern_two,
                   proj_out):
    width = target.shape[2]

    def body(top_ref, mid_ref, bot_ref, mean_ref, t_ref, n_ref, sc, k1, k2, o_ref,
             u_out, slope, hidden, d_out, d_hidden, d_g, g_two, g_out, g_one, w1, w2, w2t,
             hs, us, ds, ox, oy):
        clear_rims(hs, us, ds)
        expand(w1, k1.at[1])
        expand(w2, k2.at[1])
        expand(w2t, k2, True)
        diagonal(ox, o_ref[1])
        diagonal(oy, o_ref[1].T)
        g_two[...] = jnp.zeros(g_two.shape, F32)
        g_out[...] = jnp.zeros(g_out.shape, F32)
        g_one[...] = jnp.zeros(g_one.shape, F32)

        def entry(c):
            at = pl.ds(c, SPAN)
            for r in range(8):
                put(hs, r, c, pick(top_ref, mid_ref, bot_ref, r, at))

        def first(c):
            at = pl.ds(c, SPAN)
            rows = [near(hs, r, c) for r in range(8)]
            for r in (1, 3, 5):
                g = conv_pair(rows[r - 1 : r + 3], w1)
                for k in range(2):
                    u, s = silu(half(g, k))
                    slope[r + k - 1, at, :] = (s + u * (1.0 - s)).astype(BF16)
                    u = u.astype(BF16)
                    u_out[r + k - 1, at, :] = u
                    put(us, r + k - 1, c, u)

        def second(c):
            at = pl.ds(c, SPAN)
            rows = [near(us, r, c) for r in range(6)]
            outs, backs, hids = [], [], []
            for r in (2, 4):
                conv = conv_pair(rows[r - 2 : r + 2], w2)
                h = add_pair(mid_ref[r - 2, at, :], mid_ref[r - 1, at, :], conv)
                grads, back = finish_forward(h, r - 2, r, at, ox, oy, t_ref, n_ref, mean_ref, sc,
                                             hidden, d_out, d_hidden)
                outs += grads
                backs += back
                hids += [half(h, 0), half(h, 1)]
            for k in range(4):
                put(ds, k, c, backs[k])
            g_out[...] += dot_t(jnp.concatenate(hids, axis=0), jnp.concatenate(outs, axis=0))
            g_two[...] += kernel_grad(backs, windows(rows))

        def third(c):
            at = pl.ds(c, SPAN)
            d_u = conv_pair([near(ds, k, c) for k in range(4)], w2t)
            grads = []
            for k in range(2):
                grad = (half(d_u, k) * slope[2 + k, at, :].astype(F32)).astype(BF16)
                d_g[k, at, :] = grad
                grads.append(grad)
            g_one[...] += kernel_grad(grads, windows([near(hs, 2 + j, c) for j in range(4)]))

        spans(width, entry)
        spans(width, first)
        spans(width, second)
        spans(width, third)

    two = ((2, width, C), BF16)
    four = ((4, width, C), BF16)
    six = ((6, width, C), BF16)
    return call(
        body,
        [six, six, four, four, four, two, ((C, 9 * C), F32), ((C, C), F32), ((C, 9 * C), F32),
         WIDE, WIDE, WIDE],
        [top, middle, bottom, mean, target, noise, scalars, kern_one, kern_two, proj_out],
        [padded(8, width), padded(6, width), padded(4, width), SQUARE, SQUARE],
        LIMIT,
        10,
    )


def forward_edge(low, high, top, bottom, u_in, mean_top, mean_bottom, target, noise, scalars,
                 w_one, w_two, proj_out):
    width = target.shape[2]

    def body(lo, hi, top_ref, bot_ref, ui, mean_t, mean_b, t_ref, n_ref, sc, w1, w2, o_ref,
             u_t, u_b, sl_t, sl_b, hid_t, hid_b, do_t, do_b, dh_t, dh_b, hs, us, ox, oy):
        clear_rims(hs, us)
        diagonal(ox, o_ref[1])
        diagonal(oy, o_ref[1].T)
        edges = (top_ref, bot_ref)

        def entry(c):
            at = pl.ds(c, SPAN)
            for side in range(2):
                for k in range(2):
                    outer = (lo, hi)[side][k, at, :].astype(F32) * sc[6 + side]
                    put(hs, 6 * side + k, c, outer)
                    put(hs, 2 + 2 * side + k, c, edges[side][k, at, :])
                    put(us, 2 + 2 * side + k, c, ui[4 * side + k, at, :])

        def first(c):
            at = pl.ds(c, SPAN)
            for side in range(2):
                g = conv_pair([near(hs, 4 * side + j, c) for j in range(4)], w1)
                for k in range(2):
                    u, s = silu(half(g, k))
                    rate = s + u * (1.0 - s)
                    if k == side:
                        u = u * sc[6 + side]
                        rate = rate * sc[6 + side]
                    (sl_t, sl_b)[side][k, at, :] = rate.astype(BF16)
                    u = u.astype(BF16)
                    (u_t, u_b)[side][k, at, :] = u
                    put(us, 6 * side + k, c, u)

        def second(c):
            at = pl.ds(c, SPAN)
            for side in range(2):
                conv = conv_pair([near(us, 4 * side + j, c) for j in range(4)], w2)
                h = add_pair(edges[side][0, at, :], edges[side][1, at, :], conv)
                finish_forward(h, 0, 6 * side, at, ox, oy, t_ref, n_ref, (mean_t, mean_b)[side],
                               sc, (hid_t, hid_b)[side], (do_t, do_b)[side], (dh_t, dh_b)[side])

        spans(width, entry)
        spans(width, first)
        spans(width, second)

    two = ((2, width, C), BF16)
    return call(
        body,
        [two] * 10,
        [low, high, top, bottom, u_in, mean_top, mean_bottom, target, noise, scalars, w_one,
         w_two, proj_out],
        [padded(8, width), padded(8, width), SQUARE, SQUARE],
        LIMIT,
        6,
    )


def backward_inside(u_top, u_mid, u_bottom, slope, h_top, h_mid, h_bottom, hid_top, hid_bottom,
                    do_top, do_bottom, dh_top, dh_mid, dh_bottom, dg_mid, a_mid, coarse,
                    g_two, g_out, g_one, kern_one, w_two_t):
    width = coarse.shape[2]

    def body(ut, um, ub, sl, ht, hm, hb, hidt, hidb, dot_, dob, dht, dhm, dhb, dgm, am, c_ref,
             g2, go, g1, k1, w2t, o_two, o_out, o_one, o_in, d_g, w1t, us, hs, ds, gs):
        clear_rims(us, hs, ds, gs)
        expand(w1t, k1, True)
        o_two[...] = g2[...]
        o_out[...] = go[...]
        o_one[...] = g1[...]
        o_in[...] = jnp.zeros(o_in.shape, F32)

        def entry(c):
            at = pl.ds(c, SPAN)
            for k in range(2):
                put(us, k, c, ut[k, at, :])
                put(us, 2 + k, c, um[k, at, :])
                put(us, 4 + k, c, um[4 + k, at, :])
                put(us, 6 + k, c, ub[k, at, :])
                put(gs, 2 + k, c, dgm[k, at, :])
            for r in range(8):
                put(ds, r, c, pick(dht, dhm, dhb, r, at))
                put(hs, r, c, pick(ht, hm, hb, r, at))

        def first(c):
            at = pl.ds(c, SPAN)
            grads, groups, hids, outs = [], [], [], []
            for side, grad, hid, d_out in ((0, dht, hidt, dot_), (1, dhb, hidb, dob)):
                groups += windows([near(us, 4 * side + j, c) for j in range(4)])
                for k in range(2):
                    grads.append(grad[k, at, :])
                    hids.append(hid[k, at, :])
                    outs.append(d_out[k, at, :])
            o_two[...] += kernel_grad(grads, groups)
            o_out[...] += dot_t(jnp.concatenate(hids, axis=0), jnp.concatenate(outs, axis=0))
            for r in (1, 5):
                d_u = conv_pair([near(ds, r - 1 + j, c) for j in range(4)], w2t)
                for k in range(2):
                    rate = sl[r + k - 1, at, :].astype(F32)
                    grad = (half(d_u, k) * rate).astype(BF16)
                    d_g[(r // 5) * 2 + k, at, :] = grad
                    put(gs, r + k - 1, c, grad)

        def second(c):
            at = pl.ds(c, SPAN)
            rows = [near(hs, r, c) for r in range(8)]
            groups = windows(rows[0:4]) + windows(rows[4:8])
            o_one[...] += kernel_grad([d_g[k, at, :] for k in range(4)], groups)
            grads = [near(gs, r, c) for r in range(6)]
            zeros, joined = [], []
            for r in (2, 4):
                conv = conv_pair(grads[r - 2 : r + 2], w1t)
                d_zero = add_pair(dhm[r - 2, at, :], dhm[r - 1, at, :], conv)
                for k in range(2):
                    zeros.append(half(d_zero, k))
                    joined.append(
                        jnp.concatenate([am[r + k - 2, at, :], c_ref[0, r + k, at, :]], axis=1)
                    )
            o_in[...] += dot_t(jnp.concatenate(zeros, axis=0), jnp.concatenate(joined, axis=0))

        spans(width, entry)
        spans(width, first)
        spans(width, second)

    return call(
        body,
        [
            ((C, 9 * C), F32),
            ((C, C), F32),
            ((C, 9 * C), F32),
            ((C, 2 * C), F32),
            ((4, width, C), BF16),
            WIDE,
        ],
        [u_top, u_mid, u_bottom, slope, h_top, h_mid, h_bottom, hid_top, hid_bottom,
         do_top, do_bottom, dh_top, dh_mid, dh_bottom, dg_mid, a_mid, coarse,
         g_two, g_out, g_one, kern_one, w_two_t],
        [padded(8, width), padded(8, width), padded(8, width), padded(6, width)],
        LIMIT,
        9,
    )


def backward_edge(low, high, dh_top, dh_bottom, d_g, slope_top, slope_bottom, h_low, h_high,
                  h_top, h_bottom, a_top, a_bottom, coarse, g_two, g_out, g_one, g_in, scalars,
                  place, w_one_t, w_two_t):
    width = coarse.shape[2]

    def body(lo, hi, dht, dhb, dgi, sl_t, sl_b, hlo, hhi, ht, hb, a_t, a_b, c_ref,
             g2, go, g1, gi, sc, place_ref, w1t, w2t, keep_out, send_out,
             ds, gs, hs, own_g, one, total, flat):
        clear_rims(ds, gs, hs)
        own = (dht, dhb)
        one[...] = g1[...]
        total[...] = gi[...]

        def entry(c):
            at = pl.ds(c, SPAN)
            for side in range(2):
                keep = sc[6 + side]
                for k in range(2):
                    put(ds, 6 * side + k, c, (lo, hi)[side][k, at, :].astype(F32) * keep)
                    put(ds, 2 + 2 * side + k, c, own[side][k, at, :])
                    put(gs, 2 + 2 * side + k, c, dgi[2 * side + k, at, :])
                    put(hs, 1 + 2 * side + k, c, (ht, hb)[side][k, at, :])
                outer = (hlo, hhi)[side][1 - side, at, :].astype(F32)
                put(hs, 5 * side, c, outer * keep)

        def first(c):
            at = pl.ds(c, SPAN)
            for side in range(2):
                d_u = conv_pair([near(ds, 4 * side + j, c) for j in range(4)], w2t)
                for k in range(2):
                    rate = (sl_t, sl_b)[side][k, at, :].astype(F32)
                    grad = (half(d_u, k) * rate).astype(BF16)
                    put(gs, 6 * side + k, c, grad)
                    if k != side:
                        own_g[side, at, :] = grad

        def second(c):
            at = pl.ds(c, SPAN)
            zeros, joined, groups = [], [], []
            for side in range(2):
                groups.append([near(hs, 3 * side + j, c) for j in range(3)])
                conv = conv_pair([near(gs, 4 * side + j, c) for j in range(4)], w1t)
                d_zero = add_pair(own[side][0, at, :], own[side][1, at, :], conv)
                for k in range(2):
                    zeros.append(half(d_zero, k))
                    pair = [(a_t, a_b)[side][k, at, :], c_ref[0, 6 * side + k, at, :]]
                    joined.append(jnp.concatenate(pair, axis=1))
            one[...] += kernel_grad([own_g[0, at, :], own_g[1, at, :]], groups)
            total[...] += dot_t(jnp.concatenate(zeros, axis=0), jnp.concatenate(joined, axis=0))

        spans(width, entry)
        spans(width, first)
        spans(width, second)
        for k in range(9):
            span = slice(k * C, (k + 1) * C)
            flat[AT_ONE + k * C : AT_ONE + (k + 1) * C, :] = one[:, span].T
            flat[AT_TWO + k * C : AT_TWO + (k + 1) * C, :] = g2[:, span].T
        for k in range(2):
            flat[AT_IN + k * C : AT_IN + (k + 1) * C, :] = total[:, k * C : (k + 1) * C].T
        flat[AT_OUT : AT_OUT + C, :] = go[...]
        flat[AT_OUT + C : FLAT, :] = jnp.zeros((FLAT - AT_OUT - C, C), F32)
        part = FLAT // 2
        keep_out[...] = flat[pl.ds(pl.multiple_of(place_ref[0] * part, part), part), :]
        send_out[...] = flat[pl.ds(pl.multiple_of((1 - place_ref[0]) * part, part), part), :]

    part = ((FLAT // 2, C), F32)
    return call(
        body,
        [part, part],
        [low, high, dh_top, dh_bottom, d_g, slope_top, slope_bottom, h_low, h_high, h_top,
         h_bottom, a_top, a_bottom, coarse, g_two, g_out, g_one, g_in, scalars, place, w_one_t,
         w_two_t],
        [padded(8, width), padded(8, width), padded(6, width), pltpu.VMEM((2, width, C), BF16),
         pltpu.VMEM((C, 9 * C), F32), pltpu.VMEM((C, 2 * C), F32), pltpu.VMEM((FLAT, C), F32)],
        LIMIT,
        6,
    )


def shifted(axis, step):
    pairs = []
    for dp in range(8):
        for segment in range(2):
            for tile in range(8):
                at = {"x": tile % 4, "y": dp % 4, "z": (dp // 4) * 2 + tile // 4, "core": segment}
                to = dict(at)
                to[axis] = (at[axis] + step) % (2 if axis == "core" else 4)
                target = ((to["z"] // 2) * 4 + to["y"]) * 16 + to["core"] * 8
                target += (to["z"] % 2) * 4 + to["x"]
                pairs.append(((dp * 2 + segment) * 8 + tile, target))
    return pairs


def send(value, axis, step):
    return lax.ppermute(value, AXES, shifted(axis, step))


def scalar(value):
    return jnp.asarray(value, jnp.int32).reshape(1)


def split(terms, parts, index):
    rows = terms[0].shape[0] // parts
    count = len(terms)

    def body(*refs):
        at = refs[0]
        for j in range(parts):
            start = pl.multiple_of(lax.rem(at[0] + j, parts) * rows, 8)
            total = refs[1][pl.ds(start, rows), :]
            for term in refs[2 : 1 + count]:
                total = total + term[pl.ds(start, rows), :]
            refs[1 + count + j][...] = total

    return call(body, [((rows, C), F32)] * parts, [scalar(index), *terms], [], 8)


def join(chunks, index):
    rows = chunks[0].shape[0]
    parts = len(chunks)

    def body(*refs):
        at = refs[0]
        for j in range(parts):
            start = pl.multiple_of(lax.rem(at[0] + j, parts) * rows, 8)
            refs[-1][pl.ds(start, rows), :] = refs[1 + j][...]

    return call(body, [((rows * parts, C), F32)], [scalar(index), *chunks], [], 8)[0]


def add(terms):
    def body(*refs):
        total = refs[0][...]
        for term in refs[1:-1]:
            total = total + term[...]
        refs[-1][...] = total

    return call(body, [(terms[0].shape, F32)], terms, [], 8)[0]


def reduce_all(keep, other, core, x, y):
    got = send(other, "core", 1)
    own, *rest = split([keep, got], 4, x)
    got = [send(part, "x", j + 1) for j, part in enumerate(rest)]
    own, *rest = split([own, *got], 4, y)
    got = [send(part, "y", j + 1) for j, part in enumerate(rest)]
    own = add([own, *got])
    own = add([own, *[send(own, "z", j + 1) for j in range(3)]])
    own = join([own, *[send(own, "y", -(j + 1)) for j in range(3)]], y)
    own = join([own, *[send(own, "x", -(j + 1)) for j in range(3)]], x)
    got = send(own, "core", 1)

    def body(at, a_ref, b_ref, g_in, g_one, g_two, g_out):
        half = FLAT // 2
        first = at[0] == 0

        def rows(start, stop):
            if stop <= half:
                span = slice(start, stop)
            else:
                span = slice(start - half, stop - half)
            low = stop <= half
            return jnp.where(first == low, a_ref[span, :], b_ref[span, :])

        g_in[...] = rows(AT_IN, AT_ONE)
        g_one[...] = rows(AT_ONE, AT_TWO)
        g_two[...] = rows(AT_TWO, AT_OUT)
        g_out[...] = rows(AT_OUT, AT_OUT + C)

    return call(
        body,
        [((2 * C, C), F32), ((9 * C, C), F32), ((9 * C, C), F32), ((C, C), F32)],
        [scalar(core), own, got],
        [],
        8,
    )


def exchange(top, bottom):
    count = lax.axis_size(ROWS)
    down = [(i, (i + 1) % count) for i in range(count)]
    up = [(target, source) for source, target in down]
    return lax.ppermute(bottom, ROWS, down), lax.ppermute(top, ROWS, up)


def on_device(coarse, static_fields, target, noise, sigma, proj_in, kern_one, kern_two, proj_out):
    segment = lax.axis_index("segment")
    tile = lax.axis_index("tile")
    x = tile % 4
    y = lax.axis_index("dp") % 4
    row = lax.axis_index(ROWS)
    cells = lax.axis_size("dp") * coarse.shape[1] * lax.axis_size(ROWS) * coarse.shape[2]
    level = sigma[0]
    total_var = level * level + 1.0
    c_in = 1.0 / jnp.sqrt(total_var)
    c_out = level / jnp.sqrt(total_var)
    weight = total_var / (level * level)
    scalars = jnp.stack(
        [
            level,
            c_in,
            1.0 / total_var,
            c_out,
            2.0 * weight * c_out / cells,
            jnp.zeros((), F32),
            (row != 0).astype(F32),
            (row != lax.axis_size(ROWS) - 1).astype(F32),
        ]
    )

    r_top, r_bottom = edge_entry(coarse, static_fields, proj_in)
    low, high = exchange(r_top, r_bottom)
    u_in, mean_mid, a_mid, h_mid, w_one, w_two = mean_inside(
        r_top, r_bottom, coarse, static_fields, target, noise, scalars, proj_in, kern_one,
        kern_two, proj_out,
    )
    mean_top, mean_bottom, a_top, a_bottom, h_top, h_bottom = mean_edge(
        low, high, r_top, r_bottom, u_in, coarse, target, noise, scalars, proj_in, w_one, w_two,
        proj_out,
    )
    h_low, h_high = exchange(h_top, h_bottom)
    (u_mid, slope_mid, hid_mid, do_mid, dh_mid, dg_mid, g_two, g_out, g_one, w_one, w_two,
     w_two_t) = forward_inside(
        h_top, h_mid, h_bottom, mean_mid, target, noise, scalars, kern_one, kern_two, proj_out,
    )
    (u_top, u_bottom, slope_top, slope_bottom, hid_top, hid_bottom, do_top, do_bottom, dh_top,
     dh_bottom) = forward_edge(
        h_low, h_high, h_top, h_bottom, u_mid, mean_top, mean_bottom, target, noise, scalars,
        w_one, w_two, proj_out,
    )
    dh_low, dh_high = exchange(dh_top, dh_bottom)
    g_two, g_out, g_one, g_in, d_g, w_one_t = backward_inside(
        u_top, u_mid, u_bottom, slope_mid, h_top, h_mid, h_bottom, hid_top, hid_bottom,
        do_top, do_bottom, dh_top, dh_mid, dh_bottom, dg_mid, a_mid, coarse,
        g_two, g_out, g_one, kern_one, w_two_t,
    )
    keep, other = backward_edge(
        dh_low, dh_high, dh_top, dh_bottom, d_g, slope_top, slope_bottom, h_low, h_high,
        h_top, h_bottom, a_top, a_bottom, coarse, g_two, g_out, g_one, g_in, scalars,
        scalar(segment), w_one_t, w_two_t,
    )
    return tuple(reduce_all(keep, other, segment, x, y))


def solution(mesh):
    placed = (
        P("dp", ("segment", "tile"), None, None),
        P(("segment", "tile"), None, None),
        P("dp", ("segment", "tile"), None, None),
        P("dp", ("segment", "tile"), None, None),
        P("dp"),
        P(),
        P(),
        P(),
        P(),
    )
    return jax.shard_map(
        on_device, mesh=mesh, in_specs=placed, out_specs=(P(), P(), P(), P()), check_vma=False
    )
```

```python
import jax
import jax.numpy as jnp
from jax import lax
from jax.experimental import pallas as pl
from jax.experimental.pallas import tpu as pltpu
from jax.sharding import PartitionSpec as P

F32 = jnp.float32
BF16 = jnp.bfloat16
C = 128
AXES = ("dp", "segment", "tile")
ROWS = ("segment", "tile")
VMEM = pl.BlockSpec(memory_space=pltpu.VMEM)
SMEM = pl.BlockSpec(memory_space=pltpu.SMEM)
HBM = pl.BlockSpec(memory_space=pltpu.HBM)
MIB = 1 << 20
LIMIT = 28
ENTRY_LIMIT = 12
SPAN = 1024
AT_IN, AT_ONE, AT_TWO, AT_OUT, FLAT = 0, 256, 1408, 2560, 2816


def dot(a, b):
    return jnp.dot(a, b, preferred_element_type=F32)


def dot_t(a, b):
    return lax.dot_general(a, b, (((0,), (0,)), ((), ())), preferred_element_type=F32)


def clear_rims(*fields):
    for field in fields:
        width = field.shape[1] - 16
        for i in range(field.shape[0]):
            field[i, 0:8, :] = jnp.zeros((8, C), F32)
            field[i, width + 8 : width + 16, :] = jnp.zeros((8, C), F32)


def spans(width, body):
    @pl.loop(0, width // SPAN)
    def _(i):
        body(pl.multiple_of(i * SPAN, SPAN))


def put(field, i, c, value):
    field[i, pl.ds(pl.multiple_of(c + 8, 8), SPAN), :] = value.astype(F32)


def near(field, i, c):
    view = field.at[i, pl.ds(c, SPAN + 16), :]
    return [view[7 + k : 7 + k + SPAN, :].astype(BF16) for k in range(3)]


def expand(wx, kern, transposed=False):
    blank = jnp.zeros((C, C), BF16)
    for row in range(3):
        for col in range(3):
            if transposed:
                at = (8 - 3 * row - col) * C
                tap = kern[1, at : at + C, :].T
            else:
                at = (3 * row + col) * C
                tap = kern[at : at + C, :]
            for k in range(2):
                to = (3 * (row + k) + col) * C
                wx[to : to + C, k * C : (k + 1) * C] = tap
    for col in range(3):
        wx[(9 + col) * C : (10 + col) * C, 0:C] = blank
        wx[col * C : (col + 1) * C, C : 2 * C] = blank


def diagonal(ox, proj):
    blank = jnp.zeros((C, C), BF16)
    ox[0:C, 0:C] = proj
    ox[C : 2 * C, C : 2 * C] = proj
    ox[0:C, C : 2 * C] = blank
    ox[C : 2 * C, 0:C] = blank


def conv_pair(rows, wx):
    return dot(jnp.concatenate(rows[0] + rows[1] + rows[2] + rows[3], axis=1), wx[...])


def kernel_grad(grads, rows):
    wide = [jnp.concatenate(sum(group, []), axis=1) for group in rows]
    return dot_t(jnp.concatenate(grads, axis=0), jnp.concatenate(wide, axis=0))


def windows(rows):
    return [rows[i : i + 3] for i in range(len(rows) - 2)]


def cost(products):
    flops = 2 * 1024 * 12 * C * 2 * C * products
    return pl.CostEstimate(flops=flops, bytes_accessed=2 * MIB, transcendentals=0)


def call(body, outs, ins, scratch, limit, products=0, far=()):
    specs = [SMEM if i.ndim == 1 else VMEM for i in ins]
    for place in far:
        specs[place] = HBM
    return pl.pallas_call(
        body,
        out_shape=[jax.ShapeDtypeStruct(*o) for o in outs],
        in_specs=specs,
        out_specs=[VMEM] * len(outs),
        scratch_shapes=scratch,
        compiler_params=pltpu.CompilerParams(vmem_limit_bytes=limit * MIB),
        cost_estimate=cost(products),
    )(*ins)


def fetch(pairs, sems):
    copies = [pltpu.make_async_copy(*pair, sems.at[i]) for i, pair in enumerate(pairs)]
    for copy in copies:
        copy.start()
    return copies


def wait(copies):
    for copy in copies:
        copy.wait()


def silu(g):
    s = 0.5 * jnp.tanh(0.5 * g) + 0.5
    return g * s, s


def half(pair, k):
    return pair[:, k * C : (k + 1) * C]


def pick(top, mid, bottom, r, at):
    if r < 2:
        return top[r, at, :]
    return bottom[r - 6, at, :] if r > 5 else mid[r - 2, at, :]


def add_pair(first, second, conv):
    return jnp.concatenate(
        [
            (first.astype(F32) + half(conv, 0)).astype(BF16),
            (second.astype(F32) + half(conv, 1)).astype(BF16),
        ],
        axis=1,
    )


def padded(count, width):
    return pltpu.VMEM((count, width + 16, C), F32)


WIDE = ((12 * C, 2 * C), BF16)
SQUARE = pltpu.VMEM((2 * C, 2 * C), BF16)


def edge_entry(coarse, statics, proj_in):
    width = coarse.shape[2]

    def body(c_ref, s_ref, p_ref, top, bottom, cs, ss, ps, sems):
        pairs = [(p_ref.at[0], ps)]
        for side in range(2):
            for k in range(2):
                pairs.append((c_ref.at[0, 6 * side + k], cs.at[side, k]))
                pairs.append((s_ref.at[6 * side + k], ss.at[side, k]))
        copies = fetch(pairs, sems)
        copies[0].wait()
        for side, out in ((0, top), (1, bottom)):
            for k in range(2):
                at = 1 + 4 * side + 2 * k
                wait(copies[at : at + 2])
                both = jnp.concatenate([cs[side, k], ss[side, k]], axis=1)
                out[k] = dot(both, ps[...]).astype(BF16)

    two = ((2, width, C), BF16)
    edge = pltpu.VMEM((2, 2, width, C), BF16)
    return call(
        body,
        [two, two],
        [coarse, statics, proj_in],
        [edge, edge, pltpu.VMEM((2 * C, C), BF16), pltpu.SemaphoreType.DMA((9,))],
        ENTRY_LIMIT,
        1,
        (0, 1, 2),
    )


def finish_mean(h, i, at, ox, target, noise, coarse, sc, proj_in, mean, a, h_zero):
    both = dot(h, ox[...])
    for k in range(2):
        m = half(both, k).astype(BF16)
        mean[i + k, at, :] = m
        residual = target[i + k, at, :].astype(F32) - m.astype(F32)
        noisy = residual + sc[0] * noise[i + k, at, :].astype(F32)
        scaled = (sc[1] * noisy).astype(BF16)
        a[i + k, at, :] = scaled
        joined = jnp.concatenate([scaled, coarse[i + k, at, :]], axis=1)
        h_zero[i + k, at, :] = dot(joined, proj_in[1]).astype(BF16)


def mean_inside(top, bottom, coarse, statics, target, noise, scalars, proj_in, kern_one,
                kern_two, proj_out):
    width = coarse.shape[2]

    def body(top_ref, bot_ref, c_ref, s_ref, t_ref, n_ref, sc, p_ref, k1, k2, o_ref,
             u_out, mean, a, h_zero, w1, w2, hs, us, ox, cs, ss, ts, ns, sems):
        pairs = [(c_ref.at[0, 2:6], cs), (s_ref.at[2:6], ss)]
        pairs += [(t_ref.at[0, 2:6], ts), (n_ref.at[0, 2:6], ns)]
        copies = fetch(pairs, sems)
        clear_rims(hs, us)
        expand(w1, k1.at[0])
        expand(w2, k2.at[0])
        diagonal(ox, o_ref[0])

        def entry(c):
            at = pl.ds(c, SPAN)
            for r in range(8):
                if r in (2, 3, 4, 5):
                    both = jnp.concatenate([cs[r - 2, at, :], ss[r - 2, at, :]], axis=1)
                    put(hs, r, c, dot(both, p_ref[0]).astype(BF16))
                else:
                    put(hs, r, c, (top_ref, bot_ref)[r // 6][r % 2, at, :])

        def first(c):
            at = pl.ds(c, SPAN)
            rows = [near(hs, r, c) for r in range(8)]
            for r in (1, 3, 5):
                g = conv_pair(rows[r - 1 : r + 3], w1)
                for k in range(2):
                    u = silu(half(g, k))[0].astype(BF16)
                    put(us, r + k - 1, c, u)
                    if r != 3:
                        u_out[(r // 5) * 2 + k, at, :] = u

        def second(c):
            at = pl.ds(c, SPAN)
            rows = [near(us, r, c) for r in range(6)]
            for r in (2, 4):
                conv = conv_pair(rows[r - 2 : r + 2], w2)
                own = [hs[r + k, pl.ds(pl.multiple_of(c + 8, 8), SPAN), :] for k in range(2)]
                h = add_pair(*own, conv)
                finish_mean(h, r - 2, at, ox, ts, ns, cs, sc, p_ref, mean, a, h_zero)

        wait(copies[:2])
        spans(width, entry)
        spans(width, first)
        wait(copies[2:])
        spans(width, second)

    four = ((4, width, C), BF16)
    rows = pltpu.VMEM(*four)
    return call(
        body,
        [four, four, four, four, WIDE, WIDE],
        [top, bottom, coarse, statics, target, noise, scalars, proj_in, kern_one, kern_two,
         proj_out],
        [padded(8, width), padded(6, width), SQUARE, rows, rows, rows, rows,
         pltpu.SemaphoreType.DMA((4,))],
        LIMIT,
        6,
        (2, 3, 4, 5),
    )


def ordered(side, own, out):
    return own + out if side else out + own


def edge_rows(*fields):
    return [(field.at[0, 0:2], field.at[0, 6:8]) for field in fields]


def mean_edge(low, high, top, bottom, u_in, coarse, target, noise, scalars, proj_in, w_one, w_two,
              proj_out):
    width = coarse.shape[2]

    def body(lo, hi, top_ref, bot_ref, ui, c_ref, t_ref, n_ref, sc, p_ref, w1, w2, o_ref,
             mean_t, mean_b, a_t, a_b, hz_t, hz_b, hs, us, ox):
        cs, ts, ns = edge_rows(c_ref, t_ref, n_ref)
        clear_rims(hs, us)
        diagonal(ox, o_ref[0])
        edges = (top_ref, bot_ref)

        def entry(c):
            at = pl.ds(c, SPAN)
            for side in range(2):
                for k in range(2):
                    outer = (lo, hi)[side][k, at, :].astype(F32) * sc[6 + side]
                    put(hs, 6 * side + k, c, outer)
                    put(hs, 2 + 2 * side + k, c, edges[side][k, at, :])
                    put(us, 2 + 2 * side + k, c, ui[2 * side + k, at, :])

        def first(c):
            for side in range(2):
                rows = [near(hs, 4 * side + j, c) for j in range(4)]
                g = conv_pair(rows, w1)
                for k in range(2):
                    u, _ = silu(half(g, k))
                    if k == side:
                        u = u * sc[6 + side]
                    put(us, 6 * side + k, c, u.astype(BF16))

        def second(c):
            at = pl.ds(c, SPAN)
            for side in range(2):
                conv = conv_pair([near(us, 4 * side + j, c) for j in range(4)], w2)
                h = add_pair(edges[side][0, at, :], edges[side][1, at, :], conv)
                finish_mean(h, 0, at, ox, ts[side], ns[side], cs[side], sc, p_ref,
                            (mean_t, mean_b)[side], (a_t, a_b)[side], (hz_t, hz_b)[side])

        spans(width, entry)
        spans(width, first)
        spans(width, second)

    two = ((2, width, C), BF16)
    return call(
        body,
        [two] * 6,
        [low, high, top, bottom, u_in, coarse, target, noise, scalars, proj_in, w_one, w_two,
         proj_out],
        [padded(8, width), padded(8, width), SQUARE],
        LIMIT,
        5,
    )


def finish_forward(h, i, at, ox, oy, target, noise, mean, sc, hidden, d_out, d_hidden):
    both = dot(h, ox[...])
    grads = []
    for k in range(2):
        hidden[i + k, at, :] = half(h, k)
        residual = target[i + k, at, :].astype(F32) - mean[i + k, at, :].astype(F32)
        noisy = residual + sc[0] * noise[i + k, at, :].astype(F32)
        error = sc[2] * noisy + sc[3] * half(both, k) - residual
        grad = (sc[4] * error).astype(BF16)
        d_out[i + k, at, :] = grad
        grads.append(grad)
    back = dot(jnp.concatenate(grads, axis=1), oy[...]).astype(BF16)
    for k in range(2):
        d_hidden[i + k, at, :] = half(back, k)
    return grads, [half(back, 0), half(back, 1)]


def forward_inside(top, middle, bottom, mean, target, noise, scalars, kern_one, kern_two,
                   proj_out):
    width = target.shape[2]

    def body(top_ref, mid_ref, bot_ref, mean_ref, t_ref, n_ref, sc, k1, k2, o_ref,
             u_out, slope, hidden, d_out, d_hidden, d_g, g_two, g_out, g_one, w1, w2, w2t,
             hs, us, ds, ox, oy):
        ts, ns = t_ref.at[0, 2:6], n_ref.at[0, 2:6]
        clear_rims(hs, us, ds)
        expand(w1, k1.at[1])
        expand(w2, k2.at[1])
        expand(w2t, k2, True)
        diagonal(ox, o_ref[1])
        diagonal(oy, o_ref[1].T)
        g_two[...] = jnp.zeros(g_two.shape, F32)
        g_out[...] = jnp.zeros(g_out.shape, F32)
        g_one[...] = jnp.zeros(g_one.shape, F32)

        def entry(c):
            at = pl.ds(c, SPAN)
            for r in range(8):
                put(hs, r, c, pick(top_ref, mid_ref, bot_ref, r, at))

        def first(c):
            at = pl.ds(c, SPAN)
            rows = [near(hs, r, c) for r in range(8)]
            for r in (1, 3, 5):
                g = conv_pair(rows[r - 1 : r + 3], w1)
                for k in range(2):
                    u, s = silu(half(g, k))
                    slope[r + k - 1, at, :] = (s + u * (1.0 - s)).astype(BF16)
                    u = u.astype(BF16)
                    u_out[r + k - 1, at, :] = u
                    put(us, r + k - 1, c, u)

        def second(c):
            at = pl.ds(c, SPAN)
            rows = [near(us, r, c) for r in range(6)]
            outs, backs, hids = [], [], []
            for r in (2, 4):
                conv = conv_pair(rows[r - 2 : r + 2], w2)
                h = add_pair(mid_ref[r - 2, at, :], mid_ref[r - 1, at, :], conv)
                grads, back = finish_forward(h, r - 2, at, ox, oy, ts, ns, mean_ref, sc,
                                             hidden, d_out, d_hidden)
                outs += grads
                backs += back
                hids += [half(h, 0), half(h, 1)]
            for k in range(4):
                put(ds, k, c, backs[k])
            g_out[...] += dot_t(jnp.concatenate(hids, axis=0), jnp.concatenate(outs, axis=0))
            g_two[...] += kernel_grad(backs, windows(rows))

        def third(c):
            at = pl.ds(c, SPAN)
            d_u = conv_pair([near(ds, k, c) for k in range(4)], w2t)
            grads = []
            for k in range(2):
                grad = (half(d_u, k) * slope[2 + k, at, :].astype(F32)).astype(BF16)
                d_g[k, at, :] = grad
                grads.append(grad)
            g_one[...] += kernel_grad(grads, windows([near(hs, 2 + j, c) for j in range(4)]))

        spans(width, entry)
        spans(width, first)
        spans(width, second)
        spans(width, third)

    two = ((2, width, C), BF16)
    four = ((4, width, C), BF16)
    six = ((6, width, C), BF16)
    return call(
        body,
        [six, six, four, four, four, two, ((C, 9 * C), F32), ((C, C), F32), ((C, 9 * C), F32),
         WIDE, WIDE, WIDE],
        [top, middle, bottom, mean, target, noise, scalars, kern_one, kern_two, proj_out],
        [padded(8, width), padded(6, width), padded(4, width), SQUARE, SQUARE],
        LIMIT,
        10,
    )


def forward_edge(low, high, top, bottom, u_in, mean_top, mean_bottom, target, noise, scalars,
                 w_one, w_two, proj_out):
    width = target.shape[2]

    def body(lo, hi, top_ref, bot_ref, ui, mean_t, mean_b, t_ref, n_ref, sc, w1, w2, o_ref,
             u_t, u_b, sl_t, sl_b, hid_t, hid_b, do_t, do_b, dh_t, dh_b, hs, us, ox, oy):
        ts, ns = edge_rows(t_ref, n_ref)
        clear_rims(hs, us)
        diagonal(ox, o_ref[1])
        diagonal(oy, o_ref[1].T)
        edges = (top_ref, bot_ref)

        def entry(c):
            at = pl.ds(c, SPAN)
            for side in range(2):
                for k in range(2):
                    outer = (lo, hi)[side][k, at, :].astype(F32) * sc[6 + side]
                    put(hs, 6 * side + k, c, outer)
                    put(hs, 2 + 2 * side + k, c, edges[side][k, at, :])
                    put(us, 2 + 2 * side + k, c, ui[4 * side + k, at, :])

        def first(c):
            at = pl.ds(c, SPAN)
            for side in range(2):
                g = conv_pair([near(hs, 4 * side + j, c) for j in range(4)], w1)
                for k in range(2):
                    u, s = silu(half(g, k))
                    rate = s + u * (1.0 - s)
                    if k == side:
                        u = u * sc[6 + side]
                        rate = rate * sc[6 + side]
                    (sl_t, sl_b)[side][k, at, :] = rate.astype(BF16)
                    u = u.astype(BF16)
                    (u_t, u_b)[side][k, at, :] = u
                    put(us, 6 * side + k, c, u)

        def second(c):
            at = pl.ds(c, SPAN)
            for side in range(2):
                conv = conv_pair([near(us, 4 * side + j, c) for j in range(4)], w2)
                h = add_pair(edges[side][0, at, :], edges[side][1, at, :], conv)
                finish_forward(h, 0, at, ox, oy, ts[side], ns[side], (mean_t, mean_b)[side],
                               sc, (hid_t, hid_b)[side], (do_t, do_b)[side], (dh_t, dh_b)[side])

        spans(width, entry)
        spans(width, first)
        spans(width, second)

    two = ((2, width, C), BF16)
    return call(
        body,
        [two] * 10,
        [low, high, top, bottom, u_in, mean_top, mean_bottom, target, noise, scalars, w_one,
         w_two, proj_out],
        [padded(8, width), padded(8, width), SQUARE, SQUARE],
        LIMIT,
        6,
    )


def backward_inside(u_top, u_mid, u_bottom, slope, h_top, h_mid, h_bottom, hid_top, hid_bottom,
                    do_top, do_bottom, dh_top, dh_mid, dh_bottom, dg_mid, a_mid, coarse,
                    g_two, g_out, g_one, kern_one, w_two_t):
    width = coarse.shape[2]

    def body(ut, um, ub, sl, ht, hm, hb, hidt, hidb, dot_, dob, dht, dhm, dhb, dgm, am, c_ref,
             g2, go, g1, k1, w2t, o_two, o_out, o_one, o_in, d_g, w1t, us, hs, ds, gs):
        cs = c_ref.at[0, 2:6]
        clear_rims(us, hs, ds, gs)
        expand(w1t, k1, True)
        o_two[...] = g2[...]
        o_out[...] = go[...]
        o_one[...] = g1[...]
        o_in[...] = jnp.zeros(o_in.shape, F32)

        def entry(c):
            at = pl.ds(c, SPAN)
            for k in range(2):
                put(us, k, c, ut[k, at, :])
                put(us, 2 + k, c, um[k, at, :])
                put(us, 4 + k, c, um[4 + k, at, :])
                put(us, 6 + k, c, ub[k, at, :])
                put(gs, 2 + k, c, dgm[k, at, :])
            for r in range(8):
                put(ds, r, c, pick(dht, dhm, dhb, r, at))
                put(hs, r, c, pick(ht, hm, hb, r, at))

        def first(c):
            at = pl.ds(c, SPAN)
            grads, groups, hids, outs = [], [], [], []
            for side, grad, hid, d_out in ((0, dht, hidt, dot_), (1, dhb, hidb, dob)):
                groups += windows([near(us, 4 * side + j, c) for j in range(4)])
                for k in range(2):
                    grads.append(grad[k, at, :])
                    hids.append(hid[k, at, :])
                    outs.append(d_out[k, at, :])
            o_two[...] += kernel_grad(grads, groups)
            o_out[...] += dot_t(jnp.concatenate(hids, axis=0), jnp.concatenate(outs, axis=0))
            for r in (1, 5):
                d_u = conv_pair([near(ds, r - 1 + j, c) for j in range(4)], w2t)
                for k in range(2):
                    rate = sl[r + k - 1, at, :].astype(F32)
                    grad = (half(d_u, k) * rate).astype(BF16)
                    d_g[(r // 5) * 2 + k, at, :] = grad
                    put(gs, r + k - 1, c, grad)

        def second(c):
            at = pl.ds(c, SPAN)
            rows = [near(hs, r, c) for r in range(8)]
            groups = windows(rows[0:4]) + windows(rows[4:8])
            o_one[...] += kernel_grad([d_g[k, at, :] for k in range(4)], groups)
            grads = [near(gs, r, c) for r in range(6)]
            zeros, joined = [], []
            for r in (2, 4):
                conv = conv_pair(grads[r - 2 : r + 2], w1t)
                d_zero = add_pair(dhm[r - 2, at, :], dhm[r - 1, at, :], conv)
                for k in range(2):
                    zeros.append(half(d_zero, k))
                    joined.append(
                        jnp.concatenate([am[r + k - 2, at, :], cs[r + k - 2, at, :]], axis=1)
                    )
            o_in[...] += dot_t(jnp.concatenate(zeros, axis=0), jnp.concatenate(joined, axis=0))

        spans(width, entry)
        spans(width, first)
        spans(width, second)

    return call(
        body,
        [
            ((C, 9 * C), F32),
            ((C, C), F32),
            ((C, 9 * C), F32),
            ((C, 2 * C), F32),
            ((4, width, C), BF16),
            WIDE,
        ],
        [u_top, u_mid, u_bottom, slope, h_top, h_mid, h_bottom, hid_top, hid_bottom,
         do_top, do_bottom, dh_top, dh_mid, dh_bottom, dg_mid, a_mid, coarse,
         g_two, g_out, g_one, kern_one, w_two_t],
        [padded(8, width), padded(8, width), padded(8, width), padded(6, width)],
        LIMIT,
        9,
    )


def backward_edge(low, high, dh_top, dh_bottom, d_g, slope_top, slope_bottom, h_low, h_high,
                  h_top, h_bottom, a_top, a_bottom, coarse, g_two, g_out, g_one, g_in, scalars,
                  place, w_one_t, w_two_t):
    width = coarse.shape[2]

    def body(lo, hi, dht, dhb, dgi, sl_t, sl_b, hlo, hhi, ht, hb, a_t, a_b, c_ref,
             g2, go, g1, gi, sc, place_ref, w1t, w2t, keep_out, send_out,
             ds, gs, hs, own_g, one, total, flat):
        (cs,) = edge_rows(c_ref)
        clear_rims(ds, gs, hs)
        own = (dht, dhb)
        one[...] = g1[...]
        total[...] = gi[...]

        def entry(c):
            at = pl.ds(c, SPAN)
            for side in range(2):
                keep = sc[6 + side]
                for k in range(2):
                    put(ds, 6 * side + k, c, (lo, hi)[side][k, at, :].astype(F32) * keep)
                    put(ds, 2 + 2 * side + k, c, own[side][k, at, :])
                    put(gs, 2 + 2 * side + k, c, dgi[2 * side + k, at, :])
                    put(hs, 1 + 2 * side + k, c, (ht, hb)[side][k, at, :])
                outer = (hlo, hhi)[side][1 - side, at, :].astype(F32)
                put(hs, 5 * side, c, outer * keep)

        def first(c):
            at = pl.ds(c, SPAN)
            for side in range(2):
                d_u = conv_pair([near(ds, 4 * side + j, c) for j in range(4)], w2t)
                for k in range(2):
                    rate = (sl_t, sl_b)[side][k, at, :].astype(F32)
                    grad = (half(d_u, k) * rate).astype(BF16)
                    put(gs, 6 * side + k, c, grad)
                    if k != side:
                        own_g[side, at, :] = grad

        def second(c):
            at = pl.ds(c, SPAN)
            zeros, joined, groups = [], [], []
            for side in range(2):
                groups.append([near(hs, 3 * side + j, c) for j in range(3)])
                conv = conv_pair([near(gs, 4 * side + j, c) for j in range(4)], w1t)
                d_zero = add_pair(own[side][0, at, :], own[side][1, at, :], conv)
                for k in range(2):
                    zeros.append(half(d_zero, k))
                    pair = [(a_t, a_b)[side][k, at, :], cs[side][k, at, :]]
                    joined.append(jnp.concatenate(pair, axis=1))
            one[...] += kernel_grad([own_g[0, at, :], own_g[1, at, :]], groups)
            total[...] += dot_t(jnp.concatenate(zeros, axis=0), jnp.concatenate(joined, axis=0))

        spans(width, entry)
        spans(width, first)
        spans(width, second)
        for k in range(9):
            span = slice(k * C, (k + 1) * C)
            flat[AT_ONE + k * C : AT_ONE + (k + 1) * C, :] = one[:, span].T
            flat[AT_TWO + k * C : AT_TWO + (k + 1) * C, :] = g2[:, span].T
        for k in range(2):
            flat[AT_IN + k * C : AT_IN + (k + 1) * C, :] = total[:, k * C : (k + 1) * C].T
        flat[AT_OUT : AT_OUT + C, :] = go[...]
        flat[AT_OUT + C : FLAT, :] = jnp.zeros((FLAT - AT_OUT - C, C), F32)
        part = FLAT // 2
        keep_out[...] = flat[pl.ds(pl.multiple_of(place_ref[0] * part, part), part), :]
        send_out[...] = flat[pl.ds(pl.multiple_of((1 - place_ref[0]) * part, part), part), :]

    part = ((FLAT // 2, C), F32)
    return call(
        body,
        [part, part],
        [low, high, dh_top, dh_bottom, d_g, slope_top, slope_bottom, h_low, h_high, h_top,
         h_bottom, a_top, a_bottom, coarse, g_two, g_out, g_one, g_in, scalars, place, w_one_t,
         w_two_t],
        [padded(8, width), padded(8, width), padded(6, width), pltpu.VMEM((2, width, C), BF16),
         pltpu.VMEM((C, 9 * C), F32), pltpu.VMEM((C, 2 * C), F32), pltpu.VMEM((FLAT, C), F32)],
        LIMIT,
        6,
    )


def shifted(axis, step):
    pairs = []
    for dp in range(8):
        for segment in range(2):
            for tile in range(8):
                at = {"x": tile % 4, "y": dp % 4, "z": (dp // 4) * 2 + tile // 4, "core": segment}
                to = dict(at)
                to[axis] = (at[axis] + step) % (2 if axis == "core" else 4)
                target = ((to["z"] // 2) * 4 + to["y"]) * 16 + to["core"] * 8
                target += (to["z"] % 2) * 4 + to["x"]
                pairs.append(((dp * 2 + segment) * 8 + tile, target))
    return pairs


def send(value, axis, step):
    return lax.ppermute(value, AXES, shifted(axis, step))


def scalar(value):
    return jnp.asarray(value, jnp.int32).reshape(1)


def split(terms, parts, index):
    rows = terms[0].shape[0] // parts
    count = len(terms)

    def body(*refs):
        at = refs[0]
        for j in range(parts):
            start = pl.multiple_of(lax.rem(at[0] + j, parts) * rows, 8)
            total = refs[1][pl.ds(start, rows), :]
            for term in refs[2 : 1 + count]:
                total = total + term[pl.ds(start, rows), :]
            refs[1 + count + j][...] = total

    return call(body, [((rows, C), F32)] * parts, [scalar(index), *terms], [], 8)


def join(chunks, index):
    rows = chunks[0].shape[0]
    parts = len(chunks)

    def body(*refs):
        at = refs[0]
        for j in range(parts):
            start = pl.multiple_of(lax.rem(at[0] + j, parts) * rows, 8)
            refs[-1][pl.ds(start, rows), :] = refs[1 + j][...]

    return call(body, [((rows * parts, C), F32)], [scalar(index), *chunks], [], 8)[0]


def add(terms):
    def body(*refs):
        total = refs[0][...]
        for term in refs[1:-1]:
            total = total + term[...]
        refs[-1][...] = total

    return call(body, [(terms[0].shape, F32)], terms, [], 8)[0]


def reduce_all(keep, other, core, x, y):
    got = send(other, "core", 1)
    own, *rest = split([keep, got], 4, x)
    got = [send(part, "x", j + 1) for j, part in enumerate(rest)]
    own, *rest = split([own, *got], 4, y)
    got = [send(part, "y", j + 1) for j, part in enumerate(rest)]
    own = add([own, *got])
    own = add([own, *[send(own, "z", j + 1) for j in range(3)]])
    own = join([own, *[send(own, "y", -(j + 1)) for j in range(3)]], y)
    own = join([own, *[send(own, "x", -(j + 1)) for j in range(3)]], x)
    got = send(own, "core", 1)

    def body(at, a_ref, b_ref, g_in, g_one, g_two, g_out):
        half = FLAT // 2
        first = at[0] == 0

        def rows(start, stop):
            if stop <= half:
                span = slice(start, stop)
            else:
                span = slice(start - half, stop - half)
            low = stop <= half
            return jnp.where(first == low, a_ref[span, :], b_ref[span, :])

        g_in[...] = rows(AT_IN, AT_ONE)
        g_one[...] = rows(AT_ONE, AT_TWO)
        g_two[...] = rows(AT_TWO, AT_OUT)
        g_out[...] = rows(AT_OUT, AT_OUT + C)

    return call(
        body,
        [((2 * C, C), F32), ((9 * C, C), F32), ((9 * C, C), F32), ((C, C), F32)],
        [scalar(core), own, got],
        [],
        8,
    )


def exchange(top, bottom):
    count = lax.axis_size(ROWS)
    down = [(i, (i + 1) % count) for i in range(count)]
    up = [(target, source) for source, target in down]
    return lax.ppermute(bottom, ROWS, down), lax.ppermute(top, ROWS, up)


def on_device(coarse, static_fields, target, noise, sigma, proj_in, kern_one, kern_two, proj_out):
    far = [
        pltpu.with_memory_space_constraint(v, pltpu.HBM)
        for v in (coarse, static_fields, target, noise, proj_in)
    ]
    segment = lax.axis_index("segment")
    tile = lax.axis_index("tile")
    x = tile % 4
    y = lax.axis_index("dp") % 4
    row = lax.axis_index(ROWS)
    cells = lax.axis_size("dp") * coarse.shape[1] * lax.axis_size(ROWS) * coarse.shape[2]
    level = sigma[0]
    total_var = level * level + 1.0
    c_in = 1.0 / jnp.sqrt(total_var)
    c_out = level / jnp.sqrt(total_var)
    weight = total_var / (level * level)
    scalars = jnp.stack(
        [
            level,
            c_in,
            1.0 / total_var,
            c_out,
            2.0 * weight * c_out / cells,
            jnp.zeros((), F32),
            (row != 0).astype(F32),
            (row != lax.axis_size(ROWS) - 1).astype(F32),
        ]
    )

    r_top, r_bottom = edge_entry(far[0], far[1], far[4])
    low, high = exchange(r_top, r_bottom)
    u_in, mean_mid, a_mid, h_mid, w_one, w_two = mean_inside(
        r_top, r_bottom, *far[:4], scalars, proj_in, kern_one, kern_two, proj_out,
    )
    mean_top, mean_bottom, a_top, a_bottom, h_top, h_bottom = mean_edge(
        low, high, r_top, r_bottom, u_in, coarse, target, noise, scalars, proj_in, w_one, w_two,
        proj_out,
    )
    h_low, h_high = exchange(h_top, h_bottom)
    (u_mid, slope_mid, hid_mid, do_mid, dh_mid, dg_mid, g_two, g_out, g_one, w_one, w_two,
     w_two_t) = forward_inside(
        h_top, h_mid, h_bottom, mean_mid, target, noise, scalars, kern_one, kern_two, proj_out,
    )
    (u_top, u_bottom, slope_top, slope_bottom, hid_top, hid_bottom, do_top, do_bottom, dh_top,
     dh_bottom) = forward_edge(
        h_low, h_high, h_top, h_bottom, u_mid, mean_top, mean_bottom, target, noise, scalars,
        w_one, w_two, proj_out,
    )
    dh_low, dh_high = exchange(dh_top, dh_bottom)
    g_two, g_out, g_one, g_in, d_g, w_one_t = backward_inside(
        u_top, u_mid, u_bottom, slope_mid, h_top, h_mid, h_bottom, hid_top, hid_bottom,
        do_top, do_bottom, dh_top, dh_mid, dh_bottom, dg_mid, a_mid, coarse,
        g_two, g_out, g_one, kern_one, w_two_t,
    )
    keep, other = backward_edge(
        dh_low, dh_high, dh_top, dh_bottom, d_g, slope_top, slope_bottom, h_low, h_high,
        h_top, h_bottom, a_top, a_bottom, coarse, g_two, g_out, g_one, g_in, scalars,
        scalar(segment), w_one_t, w_two_t,
    )
    return tuple(reduce_all(keep, other, segment, x, y))


def solution(mesh):
    placed = (
        P("dp", ("segment", "tile"), None, None),
        P(("segment", "tile"), None, None),
        P("dp", ("segment", "tile"), None, None),
        P("dp", ("segment", "tile"), None, None),
        P("dp"),
        P(),
        P(),
        P(),
        P(),
    )
    return jax.shard_map(
        on_device, mesh=mesh, in_specs=placed, out_specs=(P(), P(), P(), P()), check_vma=False
    )
```

```python
import jax
import jax.numpy as jnp
from jax import lax
from jax.experimental import pallas as pl
from jax.experimental.pallas import tpu as pltpu
from jax.sharding import PartitionSpec as P

F32 = jnp.float32
BF16 = jnp.bfloat16
C = 128
AXES = ("dp", "segment", "tile")
ROWS = ("segment", "tile")
VMEM = pl.BlockSpec(memory_space=pltpu.VMEM)
SMEM = pl.BlockSpec(memory_space=pltpu.SMEM)
HBM = pl.BlockSpec(memory_space=pltpu.HBM)
MIB = 1 << 20
LIMIT = 26
ENTRY_LIMIT = 12
SPAN = 1024
AT_IN, AT_ONE, AT_TWO, AT_OUT, FLAT = 0, 256, 1408, 2560, 2816


def dot(a, b):
    return jnp.dot(a, b, preferred_element_type=F32)


def dot_t(a, b):
    return lax.dot_general(a, b, (((0,), (0,)), ((), ())), preferred_element_type=F32)


def clear_rims(*fields):
    for field in fields:
        width = field.shape[1] - 16
        for i in range(field.shape[0]):
            field[i, 0:8, :] = jnp.zeros((8, C), F32)
            field[i, width + 8 : width + 16, :] = jnp.zeros((8, C), F32)


def spans(width, body):
    @pl.loop(0, width // SPAN)
    def _(i):
        body(pl.multiple_of(i * SPAN, SPAN))


def put(field, i, c, value):
    field[i, pl.ds(pl.multiple_of(c + 8, 8), SPAN), :] = value.astype(F32)


def near(field, i, c):
    view = field.at[i, pl.ds(c, SPAN + 16), :]
    return [view[7 + k : 7 + k + SPAN, :].astype(BF16) for k in range(3)]


def expand(wx, kern, transposed=False):
    blank = jnp.zeros((C, C), BF16)
    for row in range(3):
        for col in range(3):
            if transposed:
                at = (8 - 3 * row - col) * C
                tap = kern[1, at : at + C, :].T
            else:
                at = (3 * row + col) * C
                tap = kern[at : at + C, :]
            for k in range(2):
                to = (3 * (row + k) + col) * C
                wx[to : to + C, k * C : (k + 1) * C] = tap
    for col in range(3):
        wx[(9 + col) * C : (10 + col) * C, 0:C] = blank
        wx[col * C : (col + 1) * C, C : 2 * C] = blank


def diagonal(ox, proj):
    blank = jnp.zeros((C, C), BF16)
    ox[0:C, 0:C] = proj
    ox[C : 2 * C, C : 2 * C] = proj
    ox[0:C, C : 2 * C] = blank
    ox[C : 2 * C, 0:C] = blank


def conv_pair(rows, wx):
    return dot(jnp.concatenate(rows[0] + rows[1] + rows[2] + rows[3], axis=1), wx[...])


def conv_half(rows, wx, lower):
    taps = 6 * C
    return dot(jnp.concatenate(rows[0] + rows[1], axis=1), wx[lower * taps : (lower + 1) * taps, :])


def kernel_grad(grads, rows):
    wide = [jnp.concatenate(sum(group, []), axis=1) for group in rows]
    return dot_t(jnp.concatenate(grads, axis=0), jnp.concatenate(wide, axis=0))


def windows(rows):
    return [rows[i : i + 3] for i in range(len(rows) - 2)]


def cost(products):
    flops = 2 * 1024 * 12 * C * 2 * C * products
    return pl.CostEstimate(flops=flops, bytes_accessed=2 * MIB, transcendentals=0)


def call(body, outs, ins, scratch, limit, products=0, far=()):
    specs = [SMEM if i.ndim == 1 else VMEM for i in ins]
    for place in far:
        specs[place] = HBM
    return pl.pallas_call(
        body,
        out_shape=[jax.ShapeDtypeStruct(*o) for o in outs],
        in_specs=specs,
        out_specs=[VMEM] * len(outs),
        scratch_shapes=scratch,
        compiler_params=pltpu.CompilerParams(vmem_limit_bytes=limit * MIB),
        cost_estimate=cost(products),
    )(*ins)


def fetch(pairs, sems):
    copies = [pltpu.make_async_copy(*pair, sems.at[i]) for i, pair in enumerate(pairs)]
    for copy in copies:
        copy.start()
    return copies


def wait(copies):
    for copy in copies:
        copy.wait()


def silu(g):
    s = 0.5 * jnp.tanh(0.5 * g) + 0.5
    return g * s, s


def half(pair, k):
    return pair[:, k * C : (k + 1) * C]


def pick(top, mid, bottom, r, at):
    if r < 2:
        return top[r, at, :]
    return bottom[r - 6, at, :] if r > 5 else mid[r - 2, at, :]


def add_pair(first, second, conv):
    return jnp.concatenate(
        [
            (first.astype(F32) + half(conv, 0)).astype(BF16),
            (second.astype(F32) + half(conv, 1)).astype(BF16),
        ],
        axis=1,
    )


def padded(count, width):
    return pltpu.VMEM((count, width + 16, C), F32)


WIDE = ((12 * C, 2 * C), BF16)
SQUARE = pltpu.VMEM((2 * C, 2 * C), BF16)


def edge_entry(coarse, statics, proj_in):
    width = coarse.shape[2]

    def body(c_ref, s_ref, p_ref, top, bottom, cs, ss, ps, sems):
        pairs = [(p_ref.at[0], ps)]
        for side in range(2):
            for k in range(2):
                pairs.append((c_ref.at[0, 6 * side + k], cs.at[side, k]))
                pairs.append((s_ref.at[6 * side + k], ss.at[side, k]))
        copies = fetch(pairs, sems)
        copies[0].wait()
        for side, out in ((0, top), (1, bottom)):
            for k in range(2):
                at = 1 + 4 * side + 2 * k
                wait(copies[at : at + 2])
                both = jnp.concatenate([cs[side, k], ss[side, k]], axis=1)
                out[k] = dot(both, ps[...]).astype(BF16)

    two = ((2, width, C), BF16)
    edge = pltpu.VMEM((2, 2, width, C), BF16)
    return call(
        body,
        [two, two],
        [coarse, statics, proj_in],
        [edge, edge, pltpu.VMEM((2 * C, C), BF16), pltpu.SemaphoreType.DMA((9,))],
        ENTRY_LIMIT,
        1,
        (0, 1, 2),
    )


def finish_mean(h, i, at, ox, target, noise, coarse, sc, proj_in, mean, a, h_zero):
    both = dot(h, ox[...])
    for k in range(2):
        m = half(both, k).astype(BF16)
        mean[i + k, at, :] = m
        residual = target[i + k, at, :].astype(F32) - m.astype(F32)
        noisy = residual + sc[0] * noise[i + k, at, :].astype(F32)
        scaled = (sc[1] * noisy).astype(BF16)
        a[i + k, at, :] = scaled
        joined = jnp.concatenate([scaled, coarse[i + k, at, :]], axis=1)
        h_zero[i + k, at, :] = dot(joined, proj_in[1]).astype(BF16)


def mean_inside(top, bottom, coarse, statics, target, noise, scalars, proj_in, kern_one,
                kern_two, proj_out):
    width = coarse.shape[2]

    def body(top_ref, bot_ref, c_ref, s_ref, t_ref, n_ref, sc, p_ref, k1, k2, o_ref,
             u_out, mean, a, h_zero, w1, w2, hs, us, ox, cs, ss, ts, ns, sems):
        pairs = [(c_ref.at[0, 2:6], cs), (s_ref.at[2:6], ss)]
        pairs += [(t_ref.at[0, 2:6], ts), (n_ref.at[0, 2:6], ns)]
        copies = fetch(pairs, sems)
        clear_rims(hs, us)
        expand(w1, k1.at[0])
        expand(w2, k2.at[0])
        diagonal(ox, o_ref[0])

        def entry(c):
            at = pl.ds(c, SPAN)
            for r in range(8):
                if r in (2, 3, 4, 5):
                    both = jnp.concatenate([cs[r - 2, at, :], ss[r - 2, at, :]], axis=1)
                    put(hs, r, c, dot(both, p_ref[0]).astype(BF16))
                else:
                    put(hs, r, c, (top_ref, bot_ref)[r // 6][r % 2, at, :])

        def first(c):
            at = pl.ds(c, SPAN)
            rows = [near(hs, r, c) for r in range(8)]
            for r in (1, 3, 5):
                g = conv_pair(rows[r - 1 : r + 3], w1)
                for k in range(2):
                    u = silu(half(g, k))[0].astype(BF16)
                    put(us, r + k - 1, c, u)
                    if r != 3:
                        u_out[(r // 5) * 2 + k, at, :] = u

        def second(c):
            at = pl.ds(c, SPAN)
            rows = [near(us, r, c) for r in range(6)]
            for r in (2, 4):
                conv = conv_pair(rows[r - 2 : r + 2], w2)
                own = [hs[r + k, pl.ds(pl.multiple_of(c + 8, 8), SPAN), :] for k in range(2)]
                h = add_pair(*own, conv)
                finish_mean(h, r - 2, at, ox, ts, ns, cs, sc, p_ref, mean, a, h_zero)

        wait(copies[:2])
        spans(width, entry)
        spans(width, first)
        wait(copies[2:])
        spans(width, second)

    four = ((4, width, C), BF16)
    rows = pltpu.VMEM(*four)
    return call(
        body,
        [four, four, four, four, WIDE, WIDE],
        [top, bottom, coarse, statics, target, noise, scalars, proj_in, kern_one, kern_two,
         proj_out],
        [padded(8, width), padded(6, width), SQUARE, rows, rows, rows, rows,
         pltpu.SemaphoreType.DMA((4,))],
        LIMIT,
        6,
        (2, 3, 4, 5),
    )


def ordered(side, own, out):
    return own + out if side else out + own


def edge_rows(*fields):
    return [(field.at[0, 0:2], field.at[0, 6:8]) for field in fields]


def mean_edge(low, high, top, bottom, u_in, coarse, target, noise, scalars, proj_in, w_one, w_two,
              proj_out):
    width = coarse.shape[2]

    def body(lo, hi, top_ref, bot_ref, ui, c_ref, t_ref, n_ref, sc, p_ref, w1, w2, o_ref,
             mean_t, mean_b, a_t, a_b, hz_t, hz_b, hs, us, ox):
        cs, ts, ns = edge_rows(c_ref, t_ref, n_ref)
        clear_rims(hs, us)
        diagonal(ox, o_ref[0])
        edges = (top_ref, bot_ref)

        def entry(c):
            at = pl.ds(c, SPAN)
            for side in range(2):
                for k in range(2):
                    outer = (lo, hi)[side][k, at, :].astype(F32) * sc[6 + side]
                    put(hs, 6 * side + k, c, outer)
                    put(hs, 2 + 2 * side + k, c, edges[side][k, at, :])
                    put(us, 2 + 2 * side + k, c, ui[2 * side + k, at, :])

        def first(c):
            for side in range(2):
                rows = [near(hs, 4 * side + j, c) for j in range(4)]
                g = conv_pair(rows, w1)
                for k in range(2):
                    u, _ = silu(half(g, k))
                    if k == side:
                        u = u * sc[6 + side]
                    put(us, 6 * side + k, c, u.astype(BF16))

        def second(c):
            at = pl.ds(c, SPAN)
            for side in range(2):
                conv = conv_pair([near(us, 4 * side + j, c) for j in range(4)], w2)
                h = add_pair(edges[side][0, at, :], edges[side][1, at, :], conv)
                finish_mean(h, 0, at, ox, ts[side], ns[side], cs[side], sc, p_ref,
                            (mean_t, mean_b)[side], (a_t, a_b)[side], (hz_t, hz_b)[side])

        spans(width, entry)
        spans(width, first)
        spans(width, second)

    two = ((2, width, C), BF16)
    return call(
        body,
        [two] * 6,
        [low, high, top, bottom, u_in, coarse, target, noise, scalars, proj_in, w_one, w_two,
         proj_out],
        [padded(8, width), padded(8, width), SQUARE],
        LIMIT,
        5,
    )


def finish_forward(h, i, at, ox, oy, target, noise, mean, sc, hidden, d_out, d_hidden):
    both = dot(h, ox[...])
    grads = []
    for k in range(2):
        if hidden is not None:
            hidden[i + k, at, :] = half(h, k)
        residual = target[i + k, at, :].astype(F32) - mean[i + k, at, :].astype(F32)
        noisy = residual + sc[0] * noise[i + k, at, :].astype(F32)
        error = sc[2] * noisy + sc[3] * half(both, k) - residual
        grad = (sc[4] * error).astype(BF16)
        if d_out is not None:
            d_out[i + k, at, :] = grad
        grads.append(grad)
    back = dot(jnp.concatenate(grads, axis=1), oy[...]).astype(BF16)
    for k in range(2):
        d_hidden[i + k, at, :] = half(back, k)
    return grads, [half(back, 0), half(back, 1)]


def forward_inside(top, middle, bottom, mean, target, noise, scalars, kern_one, kern_two,
                   proj_out):
    width = target.shape[2]

    def body(top_ref, mid_ref, bot_ref, mean_ref, t_ref, n_ref, sc, k1, k2, o_ref,
             u_out, slope, d_hidden, d_g, pg_t, pg_b, ph_t, ph_b, g_out, g_one, w1, w2, w2t,
             hs, us, ds, ox, oy):
        ts, ns = t_ref.at[0, 2:6], n_ref.at[0, 2:6]
        clear_rims(hs, us, ds)
        expand(w1, k1.at[1])
        expand(w2, k2.at[1])
        expand(w2t, k2, True)
        diagonal(ox, o_ref[1])
        diagonal(oy, o_ref[1].T)
        g_out[...] = jnp.zeros(g_out.shape, F32)
        g_one[...] = jnp.zeros(g_one.shape, F32)

        def entry(c):
            at = pl.ds(c, SPAN)
            for r in range(8):
                put(hs, r, c, pick(top_ref, mid_ref, bot_ref, r, at))

        def first(c):
            at = pl.ds(c, SPAN)
            rows = [near(hs, r, c) for r in range(8)]
            for r in (1, 3, 5):
                g = conv_pair(rows[r - 1 : r + 3], w1)
                for k in range(2):
                    u, s = silu(half(g, k))
                    slope[r + k - 1, at, :] = (s + u * (1.0 - s)).astype(BF16)
                    u = u.astype(BF16)
                    u_out[r + k - 1, at, :] = u
                    put(us, r + k - 1, c, u)
            pg_t[at, :] = conv_half(rows[0:2], w1, 1)
            pg_b[at, :] = conv_half(rows[6:8], w1, 0)

        def second(c):
            at = pl.ds(c, SPAN)
            rows = [near(us, r, c) for r in range(6)]
            ph_t[at, :] = conv_half(rows[0:2], w2, 1)
            ph_b[at, :] = conv_half(rows[4:6], w2, 0)
            outs, backs, hids = [], [], []
            for r in (2, 4):
                conv = conv_pair(rows[r - 2 : r + 2], w2)
                h = add_pair(mid_ref[r - 2, at, :], mid_ref[r - 1, at, :], conv)
                grads, back = finish_forward(h, r - 2, at, ox, oy, ts, ns, mean_ref, sc,
                                             None, None, d_hidden)
                outs += grads
                backs += back
                hids += [half(h, 0), half(h, 1)]
            for k in range(4):
                put(ds, k, c, backs[k])
            g_out[...] += dot_t(jnp.concatenate(hids, axis=0), jnp.concatenate(outs, axis=0))

        def third(c):
            at = pl.ds(c, SPAN)
            d_u = conv_pair([near(ds, k, c) for k in range(4)], w2t)
            grads = []
            for k in range(2):
                grad = (half(d_u, k) * slope[2 + k, at, :].astype(F32)).astype(BF16)
                d_g[k, at, :] = grad
                grads.append(grad)
            g_one[...] += kernel_grad(grads, windows([near(hs, 2 + j, c) for j in range(4)]))

        spans(width, entry)
        spans(width, first)
        spans(width, second)
        spans(width, third)

    two = ((2, width, C), BF16)
    four = ((4, width, C), BF16)
    six = ((6, width, C), BF16)
    return call(
        body,
        [six, six, four, two, *[((width, 2 * C), F32)] * 4, ((C, C), F32), ((C, 9 * C), F32),
         WIDE, WIDE, WIDE],
        [top, middle, bottom, mean, target, noise, scalars, kern_one, kern_two, proj_out],
        [padded(8, width), padded(6, width), padded(4, width), SQUARE, SQUARE],
        LIMIT,
        10,
    )


def forward_edge(low, high, top, bottom, parts, mean_top, mean_bottom, target, noise, scalars,
                 w_one, w_two, proj_out):
    width = target.shape[2]

    def body(lo, hi, top_ref, bot_ref, pg_t, pg_b, ph_t, ph_b, mean_t, mean_b, t_ref, n_ref, sc, w1, w2, o_ref,
             u_t, u_b, sl_t, sl_b, hid_t, hid_b, do_t, do_b, dh_t, dh_b, hs, us, ox, oy):
        ts, ns = edge_rows(t_ref, n_ref)
        clear_rims(hs, us)
        diagonal(ox, o_ref[1])
        diagonal(oy, o_ref[1].T)
        edges = (top_ref, bot_ref)

        def entry(c):
            at = pl.ds(c, SPAN)
            for side in range(2):
                for k in range(2):
                    outer = (lo, hi)[side][k, at, :].astype(F32) * sc[6 + side]
                    put(hs, 2 * side + k, c, outer)

        def first(c):
            at = pl.ds(c, SPAN)
            for side in range(2):
                g = conv_half([near(hs, 2 * side + j, c) for j in range(2)], w1, side)
                g = g + (pg_t, pg_b)[side][at, :]
                for k in range(2):
                    u, s = silu(half(g, k))
                    rate = s + u * (1.0 - s)
                    if k == side:
                        u = u * sc[6 + side]
                        rate = rate * sc[6 + side]
                    (sl_t, sl_b)[side][k, at, :] = rate.astype(BF16)
                    u = u.astype(BF16)
                    (u_t, u_b)[side][k, at, :] = u
                    put(us, 2 * side + k, c, u)

        def second(c):
            at = pl.ds(c, SPAN)
            for side in range(2):
                conv = conv_half([near(us, 2 * side + j, c) for j in range(2)], w2, side)
                conv = conv + (ph_t, ph_b)[side][at, :]
                h = add_pair(edges[side][0, at, :], edges[side][1, at, :], conv)
                finish_forward(h, 0, at, ox, oy, ts[side], ns[side], (mean_t, mean_b)[side],
                               sc, (hid_t, hid_b)[side], (do_t, do_b)[side], (dh_t, dh_b)[side])

        spans(width, entry)
        spans(width, first)
        spans(width, second)

    two = ((2, width, C), BF16)
    return call(
        body,
        [two] * 10,
        [low, high, top, bottom, *parts, mean_top, mean_bottom, target, noise, scalars, w_one,
         w_two, proj_out],
        [padded(4, width), padded(4, width), SQUARE, SQUARE],
        LIMIT,
        6,
    )


def backward_inside(u_top, u_mid, u_bottom, slope, h_top, h_mid, h_bottom, hid_top, hid_bottom,
                    do_top, do_bottom, dh_top, dh_mid, dh_bottom, dg_mid, a_mid, coarse,
                    g_out, g_one, kern_one, w_two_t):
    width = coarse.shape[2]

    def body(ut, um, ub, sl, ht, hm, hb, hidt, hidb, dot_, dob, dht, dhm, dhb, dgm, am, c_ref,
             go, g1, k1, w2t, o_two, o_out, o_one, o_in, pu_t, pu_b, pz_t, pz_b, w1t,
             us, hs, ds, gs, d_g):
        cs = c_ref.at[0, 2:6]
        clear_rims(us, hs, ds, gs)
        expand(w1t, k1, True)
        o_two[...] = jnp.zeros(o_two.shape, F32)
        o_out[...] = go[...]
        o_one[...] = g1[...]
        o_in[...] = jnp.zeros(o_in.shape, F32)

        def entry(c):
            at = pl.ds(c, SPAN)
            for k in range(2):
                put(us, k, c, ut[k, at, :])
                put(us, 8 + k, c, ub[k, at, :])
                put(gs, 2 + k, c, dgm[k, at, :])
            for k in range(6):
                put(us, 2 + k, c, um[k, at, :])
            for r in range(8):
                put(ds, r, c, pick(dht, dhm, dhb, r, at))
                put(hs, r, c, pick(ht, hm, hb, r, at))

        def first(c):
            at = pl.ds(c, SPAN)
            hids = [ref[k, at, :] for ref in (hidt, hidb) for k in range(2)]
            outs = [ref[k, at, :] for ref in (dot_, dob) for k in range(2)]
            for r in (0, 4):
                grads = [pick(dht, dhm, dhb, r + k, at) for k in range(4)]
                groups = windows([near(us, r + j, c) for j in range(6)])
                o_two[...] += kernel_grad(grads, groups)
            o_out[...] += dot_t(jnp.concatenate(hids, axis=0), jnp.concatenate(outs, axis=0))
            for r in (1, 5):
                d_u = conv_pair([near(ds, r - 1 + j, c) for j in range(4)], w2t)
                for k in range(2):
                    rate = sl[r + k - 1, at, :].astype(F32)
                    grad = (half(d_u, k) * rate).astype(BF16)
                    d_g[(r // 5) * 2 + k, at, :] = grad
                    put(gs, r + k - 1, c, grad)
            pu_t[at, :] = conv_half([near(ds, 0, c), near(ds, 1, c)], w2t, 1)
            pu_b[at, :] = conv_half([near(ds, 6, c), near(ds, 7, c)], w2t, 0)

        def second(c):
            at = pl.ds(c, SPAN)
            rows = [near(hs, r, c) for r in range(8)]
            groups = windows(rows[0:4]) + windows(rows[4:8])
            o_one[...] += kernel_grad([d_g[k, at, :] for k in range(4)], groups)
            grads = [near(gs, r, c) for r in range(6)]
            pz_t[at, :] = conv_half(grads[0:2], w1t, 1)
            pz_b[at, :] = conv_half(grads[4:6], w1t, 0)
            zeros, joined = [], []
            for r in (2, 4):
                conv = conv_pair(grads[r - 2 : r + 2], w1t)
                d_zero = add_pair(dhm[r - 2, at, :], dhm[r - 1, at, :], conv)
                for k in range(2):
                    zeros.append(half(d_zero, k))
                    joined.append(
                        jnp.concatenate([am[r + k - 2, at, :], cs[r + k - 2, at, :]], axis=1)
                    )
            o_in[...] += dot_t(jnp.concatenate(zeros, axis=0), jnp.concatenate(joined, axis=0))

        spans(width, entry)
        spans(width, first)
        spans(width, second)

    return call(
        body,
        [
            ((C, 9 * C), F32),
            ((C, C), F32),
            ((C, 9 * C), F32),
            ((C, 2 * C), F32),
            *[((width, 2 * C), F32)] * 4,
            WIDE,
        ],
        [u_top, u_mid, u_bottom, slope, h_top, h_mid, h_bottom, hid_top, hid_bottom,
         do_top, do_bottom, dh_top, dh_mid, dh_bottom, dg_mid, a_mid, coarse,
         g_out, g_one, kern_one, w_two_t],
        [padded(10, width), padded(8, width), padded(8, width), padded(6, width),
         pltpu.VMEM((4, width, C), BF16)],
        LIMIT,
        11,
    )


def backward_edge(low, high, dh_top, dh_bottom, parts, slope_top, slope_bottom, h_low, h_high,
                  h_top, h_bottom, a_top, a_bottom, coarse, g_two, g_out, g_one, g_in, scalars,
                  place, w_one_t, w_two_t):
    width = coarse.shape[2]

    def body(lo, hi, dht, dhb, pu_t, pu_b, pz_t, pz_b, sl_t, sl_b, hlo, hhi, ht, hb, a_t, a_b, c_ref,
             g2, go, g1, gi, sc, place_ref, w1t, w2t, keep_out, send_out,
             ds, gs, hs, own_g, one, total, flat):
        (cs,) = edge_rows(c_ref)
        clear_rims(ds, gs, hs)
        own = (dht, dhb)
        one[...] = g1[...]
        total[...] = gi[...]

        def entry(c):
            at = pl.ds(c, SPAN)
            for side in range(2):
                keep = sc[6 + side]
                for k in range(2):
                    put(ds, 2 * side + k, c, (lo, hi)[side][k, at, :].astype(F32) * keep)
                    put(hs, 1 + 2 * side + k, c, (ht, hb)[side][k, at, :])
                outer = (hlo, hhi)[side][1 - side, at, :].astype(F32)
                put(hs, 5 * side, c, outer * keep)

        def first(c):
            at = pl.ds(c, SPAN)
            for side in range(2):
                d_u = conv_half([near(ds, 2 * side + j, c) for j in range(2)], w2t, side)
                d_u = d_u + (pu_t, pu_b)[side][at, :]
                for k in range(2):
                    rate = (sl_t, sl_b)[side][k, at, :].astype(F32)
                    grad = (half(d_u, k) * rate).astype(BF16)
                    put(gs, 2 * side + k, c, grad)
                    if k != side:
                        own_g[side, at, :] = grad

        def second(c):
            at = pl.ds(c, SPAN)
            zeros, joined, groups = [], [], []
            for side in range(2):
                groups.append([near(hs, 3 * side + j, c) for j in range(3)])
                conv = conv_half([near(gs, 2 * side + j, c) for j in range(2)], w1t, side)
                conv = conv + (pz_t, pz_b)[side][at, :]
                d_zero = add_pair(own[side][0, at, :], own[side][1, at, :], conv)
                for k in range(2):
                    zeros.append(half(d_zero, k))
                    pair = [(a_t, a_b)[side][k, at, :], cs[side][k, at, :]]
                    joined.append(jnp.concatenate(pair, axis=1))
            one[...] += kernel_grad([own_g[0, at, :], own_g[1, at, :]], groups)
            total[...] += dot_t(jnp.concatenate(zeros, axis=0), jnp.concatenate(joined, axis=0))

        spans(width, entry)
        spans(width, first)
        spans(width, second)
        for k in range(9):
            span = slice(k * C, (k + 1) * C)
            flat[AT_ONE + k * C : AT_ONE + (k + 1) * C, :] = one[:, span].T
            flat[AT_TWO + k * C : AT_TWO + (k + 1) * C, :] = g2[:, span].T
        for k in range(2):
            flat[AT_IN + k * C : AT_IN + (k + 1) * C, :] = total[:, k * C : (k + 1) * C].T
        flat[AT_OUT : AT_OUT + C, :] = go[...]
        flat[AT_OUT + C : FLAT, :] = jnp.zeros((FLAT - AT_OUT - C, C), F32)
        part = FLAT // 2
        keep_out[...] = flat[pl.ds(pl.multiple_of(place_ref[0] * part, part), part), :]
        send_out[...] = flat[pl.ds(pl.multiple_of((1 - place_ref[0]) * part, part), part), :]

    part = ((FLAT // 2, C), F32)
    return call(
        body,
        [part, part],
        [low, high, dh_top, dh_bottom, *parts, slope_top, slope_bottom, h_low, h_high, h_top,
         h_bottom, a_top, a_bottom, coarse, g_two, g_out, g_one, g_in, scalars, place, w_one_t,
         w_two_t],
        [padded(4, width), padded(4, width), padded(6, width), pltpu.VMEM((2, width, C), BF16),
         pltpu.VMEM((C, 9 * C), F32), pltpu.VMEM((C, 2 * C), F32), pltpu.VMEM((FLAT, C), F32)],
        LIMIT,
        6,
    )


CORES = ("core", "core")
STAGES = (("x", "y"), ("y", "z"), ("z", "x"))


def shifted(axes, step):
    pairs = []
    for dp in range(8):
        for segment in range(2):
            for tile in range(8):
                at = {"x": tile % 4, "y": dp % 4, "z": (dp // 4) * 2 + tile // 4, "core": segment}
                axis = axes[segment]
                to = dict(at)
                to[axis] = (at[axis] + step) % (2 if axis == "core" else 4)
                target = ((to["z"] // 2) * 4 + to["y"]) * 16 + to["core"] * 8
                target += (to["z"] % 2) * 4 + to["x"]
                pairs.append(((dp * 2 + segment) * 8 + tile, target))
    return pairs


def send(value, axes, step):
    return lax.ppermute(value, AXES, shifted(axes, step))


def scalar(value):
    return jnp.asarray(value, jnp.int32).reshape(1)


def split(terms, parts, index):
    rows = terms[0].shape[0] // parts
    count = len(terms)

    def body(*refs):
        at = refs[0]
        for j in range(parts):
            start = pl.multiple_of(lax.rem(at[0] + j, parts) * rows, 8)
            total = refs[1][pl.ds(start, rows), :]
            for term in refs[2 : 1 + count]:
                total = total + term[pl.ds(start, rows), :]
            refs[1 + count + j][...] = total

    return call(body, [((rows, C), F32)] * parts, [scalar(index), *terms], [], 8)


def join(chunks, index):
    rows = chunks[0].shape[0]
    parts = len(chunks)

    def body(*refs):
        at = refs[0]
        for j in range(parts):
            start = pl.multiple_of(lax.rem(at[0] + j, parts) * rows, 8)
            refs[-1][pl.ds(start, rows), :] = refs[1 + j][...]

    return call(body, [((rows * parts, C), F32)], [scalar(index), *chunks], [], 8)[0]


def add(terms):
    def body(*refs):
        total = refs[0][...]
        for term in refs[1:-1]:
            total = total + term[...]
        refs[-1][...] = total

    return call(body, [(terms[0].shape, F32)], terms, [], 8)[0]


def reduce_all(keep, other, core, first, second):
    one, two, three = STAGES
    got = send(other, CORES, 1)
    own, *rest = split([keep, got], 4, first)
    got = [send(part, one, j + 1) for j, part in enumerate(rest)]
    own, *rest = split([own, *got], 4, second)
    got = [send(part, two, j + 1) for j, part in enumerate(rest)]
    own = add([own, *got])
    own = add([own, *[send(own, three, j + 1) for j in range(3)]])
    own = join([own, *[send(own, two, -(j + 1)) for j in range(3)]], second)
    own = join([own, *[send(own, one, -(j + 1)) for j in range(3)]], first)
    got = send(own, CORES, 1)

    def body(at, a_ref, b_ref, g_in, g_one, g_two, g_out):
        half = FLAT // 2
        first = at[0] == 0

        def rows(start, stop):
            if stop <= half:
                span = slice(start, stop)
            else:
                span = slice(start - half, stop - half)
            low = stop <= half
            return jnp.where(first == low, a_ref[span, :], b_ref[span, :])

        g_in[...] = rows(AT_IN, AT_ONE)
        g_one[...] = rows(AT_ONE, AT_TWO)
        g_two[...] = rows(AT_TWO, AT_OUT)
        g_out[...] = rows(AT_OUT, AT_OUT + C)

    return call(
        body,
        [((2 * C, C), F32), ((9 * C, C), F32), ((9 * C, C), F32), ((C, C), F32)],
        [scalar(core), own, got],
        [],
        8,
    )


def exchange(top, bottom):
    count = lax.axis_size(ROWS)
    down = [(i, (i + 1) % count) for i in range(count)]
    up = [(target, source) for source, target in down]
    return lax.ppermute(bottom, ROWS, down), lax.ppermute(top, ROWS, up)


def on_device(coarse, static_fields, target, noise, sigma, proj_in, kern_one, kern_two, proj_out):
    far = [
        pltpu.with_memory_space_constraint(v, pltpu.HBM)
        for v in (coarse, static_fields, target, noise, proj_in)
    ]
    segment = lax.axis_index("segment")
    tile = lax.axis_index("tile")
    x = tile % 4
    y = lax.axis_index("dp") % 4
    z = lax.axis_index("dp") // 4 * 2 + tile // 4
    row = lax.axis_index(ROWS)
    cells = lax.axis_size("dp") * coarse.shape[1] * lax.axis_size(ROWS) * coarse.shape[2]
    level = sigma[0]
    total_var = level * level + 1.0
    c_in = 1.0 / jnp.sqrt(total_var)
    c_out = level / jnp.sqrt(total_var)
    weight = total_var / (level * level)
    scalars = jnp.stack(
        [
            level,
            c_in,
            1.0 / total_var,
            c_out,
            2.0 * weight * c_out / cells,
            jnp.zeros((), F32),
            (row != 0).astype(F32),
            (row != lax.axis_size(ROWS) - 1).astype(F32),
        ]
    )

    r_top, r_bottom = edge_entry(far[0], far[1], far[4])
    low, high = exchange(r_top, r_bottom)
    u_in, mean_mid, a_mid, h_mid, w_one, w_two = mean_inside(
        r_top, r_bottom, *far[:4], scalars, proj_in, kern_one, kern_two, proj_out,
    )
    mean_top, mean_bottom, a_top, a_bottom, h_top, h_bottom = mean_edge(
        low, high, r_top, r_bottom, u_in, coarse, target, noise, scalars, proj_in, w_one, w_two,
        proj_out,
    )
    h_low, h_high = exchange(h_top, h_bottom)
    (u_mid, slope_mid, dh_mid, dg_mid, *parts, g_out, g_one, w_one, w_two,
     w_two_t) = forward_inside(
        h_top, h_mid, h_bottom, mean_mid, target, noise, scalars, kern_one, kern_two, proj_out,
    )
    (u_top, u_bottom, slope_top, slope_bottom, hid_top, hid_bottom, do_top, do_bottom, dh_top,
     dh_bottom) = forward_edge(
        h_low, h_high, h_top, h_bottom, parts, mean_top, mean_bottom, target, noise, scalars,
        w_one, w_two, proj_out,
    )
    dh_low, dh_high = exchange(dh_top, dh_bottom)
    g_two, g_out, g_one, g_in, *parts, w_one_t = backward_inside(
        u_top, u_mid, u_bottom, slope_mid, h_top, h_mid, h_bottom, hid_top, hid_bottom,
        do_top, do_bottom, dh_top, dh_mid, dh_bottom, dg_mid, a_mid, coarse,
        g_out, g_one, kern_one, w_two_t,
    )
    keep, other = backward_edge(
        dh_low, dh_high, dh_top, dh_bottom, parts, slope_top, slope_bottom, h_low, h_high,
        h_top, h_bottom, a_top, a_bottom, coarse, g_two, g_out, g_one, g_in, scalars,
        scalar(segment), w_one_t, w_two_t,
    )
    first = jnp.where(segment == 0, x, y)
    second = jnp.where(segment == 0, y, z)
    return tuple(reduce_all(keep, other, segment, first, second))


def solution(mesh):
    placed = (
        P("dp", ("segment", "tile"), None, None),
        P(("segment", "tile"), None, None),
        P("dp", ("segment", "tile"), None, None),
        P("dp", ("segment", "tile"), None, None),
        P("dp"),
        P(),
        P(),
        P(),
        P(),
    )
    return jax.shard_map(
        on_device, mesh=mesh, in_specs=placed, out_specs=(P(), P(), P(), P()), check_vma=False
    )
```

```python
import jax
import jax.numpy as jnp
from jax import lax
from jax.experimental import pallas as pl
from jax.experimental.pallas import tpu as pltpu
from jax.sharding import PartitionSpec as P

F32 = jnp.float32
BF16 = jnp.bfloat16
C = 128
AXES = ("dp", "segment", "tile")
ROWS = ("segment", "tile")
VMEM = pl.BlockSpec(memory_space=pltpu.VMEM)
SMEM = pl.BlockSpec(memory_space=pltpu.SMEM)
HBM = pl.BlockSpec(memory_space=pltpu.HBM)
MIB = 1 << 20
LIMIT = 26
ENTRY_LIMIT = 12
SPAN = 1024
AT_IN, AT_ONE, AT_TWO, AT_OUT, FLAT = 0, 256, 1408, 2560, 2816


def dot(a, b):
    return jnp.dot(a, b, preferred_element_type=F32)


def dot_t(a, b):
    return lax.dot_general(a, b, (((0,), (0,)), ((), ())), preferred_element_type=F32)


def clear_rims(*fields):
    for field in fields:
        width = field.shape[1] - 16
        for i in range(field.shape[0]):
            field[i, 0:8, :] = jnp.zeros((8, C), F32)
            field[i, width + 8 : width + 16, :] = jnp.zeros((8, C), F32)


def spans(width, body):
    @pl.loop(0, width // SPAN)
    def _(i):
        body(pl.multiple_of(i * SPAN, SPAN))


def put(field, i, c, value):
    field[i, pl.ds(pl.multiple_of(c + 8, 8), SPAN), :] = value.astype(F32)


def near(field, i, c):
    view = field.at[i, pl.ds(c, SPAN + 16), :]
    return [view[7 + k : 7 + k + SPAN, :].astype(BF16) for k in range(3)]


def expand(wx, kern, transposed=False):
    blank = jnp.zeros((C, C), BF16)
    for row in range(3):
        for col in range(3):
            if transposed:
                at = (8 - 3 * row - col) * C
                tap = kern[1, at : at + C, :].T
            else:
                at = (3 * row + col) * C
                tap = kern[at : at + C, :]
            for k in range(2):
                to = (3 * (row + k) + col) * C
                wx[to : to + C, k * C : (k + 1) * C] = tap
    for col in range(3):
        wx[(9 + col) * C : (10 + col) * C, 0:C] = blank
        wx[col * C : (col + 1) * C, C : 2 * C] = blank


def diagonal(ox, proj):
    blank = jnp.zeros((C, C), BF16)
    ox[0:C, 0:C] = proj
    ox[C : 2 * C, C : 2 * C] = proj
    ox[0:C, C : 2 * C] = blank
    ox[C : 2 * C, 0:C] = blank


def conv_pair(rows, wx):
    return dot(jnp.concatenate(rows[0] + rows[1] + rows[2] + rows[3], axis=1), wx[...])


def conv_half(rows, wx, lower):
    taps = 6 * C
    return dot(jnp.concatenate(rows[0] + rows[1], axis=1), wx[lower * taps : (lower + 1) * taps, :])


def kernel_grad(grads, rows):
    wide = [jnp.concatenate(sum(group, []), axis=1) for group in rows]
    return dot_t(jnp.concatenate(grads, axis=0), jnp.concatenate(wide, axis=0))


def windows(rows):
    return [rows[i : i + 3] for i in range(len(rows) - 2)]


def cost(products):
    flops = 2 * 1024 * 12 * C * 2 * C * products
    return pl.CostEstimate(flops=flops, bytes_accessed=2 * MIB, transcendentals=0)


def call(body, outs, ins, scratch, limit, products=0, far=()):
    specs = [SMEM if i.ndim == 1 else VMEM for i in ins]
    for place in far:
        specs[place] = HBM
    return pl.pallas_call(
        body,
        out_shape=[jax.ShapeDtypeStruct(*o) for o in outs],
        in_specs=specs,
        out_specs=[VMEM] * len(outs),
        scratch_shapes=scratch,
        compiler_params=pltpu.CompilerParams(vmem_limit_bytes=limit * MIB),
        cost_estimate=cost(products),
    )(*ins)


def fetch(pairs, sems):
    copies = [pltpu.make_async_copy(*pair, sems.at[i]) for i, pair in enumerate(pairs)]
    for copy in copies:
        copy.start()
    return copies


def wait(copies):
    for copy in copies:
        copy.wait()


def silu(g):
    s = 0.5 * jnp.tanh(0.5 * g) + 0.5
    return g * s, s


def half(pair, k):
    return pair[:, k * C : (k + 1) * C]


def pick(top, mid, bottom, r, at):
    if r < 2:
        return top[r, at, :]
    return bottom[r - 6, at, :] if r > 5 else mid[r - 2, at, :]


def add_pair(first, second, conv):
    return jnp.concatenate(
        [
            (first.astype(F32) + half(conv, 0)).astype(BF16),
            (second.astype(F32) + half(conv, 1)).astype(BF16),
        ],
        axis=1,
    )


def padded(count, width):
    return pltpu.VMEM((count, width + 16, C), F32)


WIDE = ((12 * C, 2 * C), BF16)
SQUARE = pltpu.VMEM((2 * C, 2 * C), BF16)


def edge_entry(coarse, statics, proj_in):
    width = coarse.shape[2]

    def body(c_ref, s_ref, p_ref, top, bottom, cs, ss, ps, sems):
        pairs = [(p_ref.at[0], ps)]
        for side in range(2):
            for k in range(2):
                pairs.append((c_ref.at[0, 6 * side + k], cs.at[side, k]))
                pairs.append((s_ref.at[6 * side + k], ss.at[side, k]))
        copies = fetch(pairs, sems)
        copies[0].wait()
        for side, out in ((0, top), (1, bottom)):
            for k in range(2):
                at = 1 + 4 * side + 2 * k
                wait(copies[at : at + 2])
                both = jnp.concatenate([cs[side, k], ss[side, k]], axis=1)
                out[k] = dot(both, ps[...]).astype(BF16)

    two = ((2, width, C), BF16)
    edge = pltpu.VMEM((2, 2, width, C), BF16)
    return call(
        body,
        [two, two],
        [coarse, statics, proj_in],
        [edge, edge, pltpu.VMEM((2 * C, C), BF16), pltpu.SemaphoreType.DMA((9,))],
        ENTRY_LIMIT,
        1,
        (0, 1, 2),
    )


def finish_mean(h, i, at, ox, target, noise, coarse, sc, proj_in, mean, a, h_zero):
    both = dot(h, ox[...])
    for k in range(2):
        m = half(both, k).astype(BF16)
        mean[i + k, at, :] = m
        residual = target[i + k, at, :].astype(F32) - m.astype(F32)
        noisy = residual + sc[0] * noise[i + k, at, :].astype(F32)
        scaled = (sc[1] * noisy).astype(BF16)
        a[i + k, at, :] = scaled
        joined = jnp.concatenate([scaled, coarse[i + k, at, :]], axis=1)
        h_zero[i + k, at, :] = dot(joined, proj_in[1]).astype(BF16)


def mean_inside(top, bottom, coarse, statics, target, noise, scalars, proj_in, kern_one,
                kern_two, proj_out):
    width = coarse.shape[2]

    def body(top_ref, bot_ref, c_ref, s_ref, t_ref, n_ref, sc, p_ref, k1, k2, o_ref,
             u_out, mean, a, h_zero, w1, w2, hs, us, ox, cs, ss, ts, ns, sems):
        pairs = [(c_ref.at[0, 2:6], cs), (s_ref.at[2:6], ss)]
        pairs += [(t_ref.at[0, 2:6], ts), (n_ref.at[0, 2:6], ns)]
        copies = fetch(pairs, sems)
        clear_rims(hs, us)
        expand(w1, k1.at[0])
        expand(w2, k2.at[0])
        diagonal(ox, o_ref[0])

        def entry(c):
            at = pl.ds(c, SPAN)
            for r in range(8):
                if r in (2, 3, 4, 5):
                    both = jnp.concatenate([cs[r - 2, at, :], ss[r - 2, at, :]], axis=1)
                    put(hs, r, c, dot(both, p_ref[0]).astype(BF16))
                else:
                    put(hs, r, c, (top_ref, bot_ref)[r // 6][r % 2, at, :])

        def first(c):
            at = pl.ds(c, SPAN)
            rows = [near(hs, r, c) for r in range(8)]
            for r in (1, 3, 5):
                g = conv_pair(rows[r - 1 : r + 3], w1)
                for k in range(2):
                    u = silu(half(g, k))[0].astype(BF16)
                    put(us, r + k - 1, c, u)
                    if r != 3:
                        u_out[(r // 5) * 2 + k, at, :] = u

        def second(c):
            at = pl.ds(c, SPAN)
            rows = [near(us, r, c) for r in range(6)]
            for r in (2, 4):
                conv = conv_pair(rows[r - 2 : r + 2], w2)
                own = [hs[r + k, pl.ds(pl.multiple_of(c + 8, 8), SPAN), :] for k in range(2)]
                h = add_pair(*own, conv)
                finish_mean(h, r - 2, at, ox, ts, ns, cs, sc, p_ref, mean, a, h_zero)

        wait(copies[:2])
        spans(width, entry)
        spans(width, first)
        wait(copies[2:])
        spans(width, second)

    four = ((4, width, C), BF16)
    rows = pltpu.VMEM(*four)
    return call(
        body,
        [four, four, four, four, WIDE, WIDE],
        [top, bottom, coarse, statics, target, noise, scalars, proj_in, kern_one, kern_two,
         proj_out],
        [padded(8, width), padded(6, width), SQUARE, rows, rows, rows, rows,
         pltpu.SemaphoreType.DMA((4,))],
        LIMIT,
        6,
        (2, 3, 4, 5),
    )


def ordered(side, own, out):
    return own + out if side else out + own


def edge_rows(*fields):
    return [(field.at[0, 0:2], field.at[0, 6:8]) for field in fields]


def mean_edge(low, high, top, bottom, u_in, coarse, target, noise, scalars, proj_in, w_one, w_two,
              proj_out):
    width = coarse.shape[2]

    def body(lo, hi, top_ref, bot_ref, ui, c_ref, t_ref, n_ref, sc, p_ref, w1, w2, o_ref,
             mean_t, mean_b, a_t, a_b, hz_t, hz_b, hs, us, ox):
        cs, ts, ns = edge_rows(c_ref, t_ref, n_ref)
        clear_rims(hs, us)
        diagonal(ox, o_ref[0])
        edges = (top_ref, bot_ref)

        def entry(c):
            at = pl.ds(c, SPAN)
            for side in range(2):
                for k in range(2):
                    outer = (lo, hi)[side][k, at, :].astype(F32) * sc[6 + side]
                    put(hs, 6 * side + k, c, outer)
                    put(hs, 2 + 2 * side + k, c, edges[side][k, at, :])
                    put(us, 2 + 2 * side + k, c, ui[2 * side + k, at, :])

        def first(c):
            for side in range(2):
                rows = [near(hs, 4 * side + j, c) for j in range(4)]
                g = conv_pair(rows, w1)
                for k in range(2):
                    u, _ = silu(half(g, k))
                    if k == side:
                        u = u * sc[6 + side]
                    put(us, 6 * side + k, c, u.astype(BF16))

        def second(c):
            at = pl.ds(c, SPAN)
            for side in range(2):
                conv = conv_pair([near(us, 4 * side + j, c) for j in range(4)], w2)
                h = add_pair(edges[side][0, at, :], edges[side][1, at, :], conv)
                finish_mean(h, 0, at, ox, ts[side], ns[side], cs[side], sc, p_ref,
                            (mean_t, mean_b)[side], (a_t, a_b)[side], (hz_t, hz_b)[side])

        spans(width, entry)
        spans(width, first)
        spans(width, second)

    two = ((2, width, C), BF16)
    return call(
        body,
        [two] * 6,
        [low, high, top, bottom, u_in, coarse, target, noise, scalars, proj_in, w_one, w_two,
         proj_out],
        [padded(8, width), padded(8, width), SQUARE],
        LIMIT,
        5,
    )


def finish_forward(h, i, at, ox, oy, target, noise, mean, sc, hidden, d_out, d_hidden):
    both = dot(h, ox[...])
    grads = []
    for k in range(2):
        if hidden is not None:
            hidden[i + k, at, :] = half(h, k)
        residual = target[i + k, at, :].astype(F32) - mean[i + k, at, :].astype(F32)
        noisy = residual + sc[0] * noise[i + k, at, :].astype(F32)
        error = sc[2] * noisy + sc[3] * half(both, k) - residual
        grad = (sc[4] * error).astype(BF16)
        if d_out is not None:
            d_out[i + k, at, :] = grad
        grads.append(grad)
    back = dot(jnp.concatenate(grads, axis=1), oy[...]).astype(BF16)
    for k in range(2):
        d_hidden[i + k, at, :] = half(back, k)
    return grads, [half(back, 0), half(back, 1)]


def forward_inside(top, middle, bottom, mean, target, noise, scalars, kern_one, kern_two,
                   proj_out):
    width = target.shape[2]

    def body(top_ref, mid_ref, bot_ref, mean_ref, t_ref, n_ref, sc, k1, k2, o_ref,
             u_out, slope, d_hidden, d_g, pg_t, pg_b, ph_t, ph_b, g_out, w1, w2, w2t,
             hs, us, ds, ox, oy):
        ts, ns = t_ref.at[0, 2:6], n_ref.at[0, 2:6]
        clear_rims(hs, us, ds)
        expand(w1, k1.at[1])
        expand(w2, k2.at[1])
        expand(w2t, k2, True)
        diagonal(ox, o_ref[1])
        diagonal(oy, o_ref[1].T)
        g_out[...] = jnp.zeros(g_out.shape, F32)

        def entry(c):
            at = pl.ds(c, SPAN)
            for r in range(8):
                put(hs, r, c, pick(top_ref, mid_ref, bot_ref, r, at))

        def first(c):
            at = pl.ds(c, SPAN)
            rows = [near(hs, r, c) for r in range(8)]
            for r in (1, 3, 5):
                g = conv_pair(rows[r - 1 : r + 3], w1)
                for k in range(2):
                    u, s = silu(half(g, k))
                    slope[r + k - 1, at, :] = (s + u * (1.0 - s)).astype(BF16)
                    u = u.astype(BF16)
                    u_out[r + k - 1, at, :] = u
                    put(us, r + k - 1, c, u)
            pg_t[at, :] = conv_half(rows[0:2], w1, 1)
            pg_b[at, :] = conv_half(rows[6:8], w1, 0)

        def second(c):
            at = pl.ds(c, SPAN)
            rows = [near(us, r, c) for r in range(6)]
            ph_t[at, :] = conv_half(rows[0:2], w2, 1)
            ph_b[at, :] = conv_half(rows[4:6], w2, 0)
            outs, backs, hids = [], [], []
            for r in (2, 4):
                conv = conv_pair(rows[r - 2 : r + 2], w2)
                h = add_pair(mid_ref[r - 2, at, :], mid_ref[r - 1, at, :], conv)
                grads, back = finish_forward(h, r - 2, at, ox, oy, ts, ns, mean_ref, sc,
                                             None, None, d_hidden)
                outs += grads
                backs += back
                hids += [half(h, 0), half(h, 1)]
            for k in range(4):
                put(ds, k, c, backs[k])
            g_out[...] += dot_t(jnp.concatenate(hids, axis=0), jnp.concatenate(outs, axis=0))

        def third(c):
            at = pl.ds(c, SPAN)
            d_u = conv_pair([near(ds, k, c) for k in range(4)], w2t)
            for k in range(2):
                rate = slope[2 + k, at, :].astype(F32)
                d_g[k, at, :] = (half(d_u, k) * rate).astype(BF16)

        spans(width, entry)
        spans(width, first)
        spans(width, second)
        spans(width, third)

    two = ((2, width, C), BF16)
    four = ((4, width, C), BF16)
    six = ((6, width, C), BF16)
    return call(
        body,
        [six, six, four, two, *[((width, 2 * C), F32)] * 4, ((C, C), F32), WIDE, WIDE, WIDE],
        [top, middle, bottom, mean, target, noise, scalars, kern_one, kern_two, proj_out],
        [padded(8, width), padded(6, width), padded(4, width), SQUARE, SQUARE],
        LIMIT,
        10,
    )


def forward_edge(low, high, top, bottom, parts, mean_top, mean_bottom, target, noise, scalars,
                 w_one, w_two, proj_out):
    width = target.shape[2]

    def body(lo, hi, top_ref, bot_ref, pg_t, pg_b, ph_t, ph_b, mean_t, mean_b, t_ref, n_ref, sc, w1, w2, o_ref,
             u_t, u_b, sl_t, sl_b, hid_t, hid_b, do_t, do_b, dh_t, dh_b, hs, us, ox, oy):
        ts, ns = edge_rows(t_ref, n_ref)
        clear_rims(hs, us)
        diagonal(ox, o_ref[1])
        diagonal(oy, o_ref[1].T)
        edges = (top_ref, bot_ref)

        def entry(c):
            at = pl.ds(c, SPAN)
            for side in range(2):
                for k in range(2):
                    outer = (lo, hi)[side][k, at, :].astype(F32) * sc[6 + side]
                    put(hs, 2 * side + k, c, outer)

        def first(c):
            at = pl.ds(c, SPAN)
            for side in range(2):
                g = conv_half([near(hs, 2 * side + j, c) for j in range(2)], w1, side)
                g = g + (pg_t, pg_b)[side][at, :]
                for k in range(2):
                    u, s = silu(half(g, k))
                    rate = s + u * (1.0 - s)
                    if k == side:
                        u = u * sc[6 + side]
                        rate = rate * sc[6 + side]
                    (sl_t, sl_b)[side][k, at, :] = rate.astype(BF16)
                    u = u.astype(BF16)
                    (u_t, u_b)[side][k, at, :] = u
                    put(us, 2 * side + k, c, u)

        def second(c):
            at = pl.ds(c, SPAN)
            for side in range(2):
                conv = conv_half([near(us, 2 * side + j, c) for j in range(2)], w2, side)
                conv = conv + (ph_t, ph_b)[side][at, :]
                h = add_pair(edges[side][0, at, :], edges[side][1, at, :], conv)
                finish_forward(h, 0, at, ox, oy, ts[side], ns[side], (mean_t, mean_b)[side],
                               sc, (hid_t, hid_b)[side], (do_t, do_b)[side], (dh_t, dh_b)[side])

        spans(width, entry)
        spans(width, first)
        spans(width, second)

    two = ((2, width, C), BF16)
    return call(
        body,
        [two] * 10,
        [low, high, top, bottom, *parts, mean_top, mean_bottom, target, noise, scalars, w_one,
         w_two, proj_out],
        [padded(4, width), padded(4, width), SQUARE, SQUARE],
        LIMIT,
        6,
    )


def backward_inside(u_top, u_mid, u_bottom, slope, h_top, h_mid, h_bottom, hid_top, hid_bottom,
                    do_top, do_bottom, dh_top, dh_mid, dh_bottom, dg_mid, a_mid, coarse,
                    g_out, kern_one, w_two_t):
    width = coarse.shape[2]

    def body(ut, um, ub, sl, ht, hm, hb, hidt, hidb, dot_, dob, dht, dhm, dhb, dgm, am, c_ref,
             go, k1, w2t, o_two, o_out, o_one, o_in, pu_t, pu_b, pz_t, pz_b, w1t,
             us, hs, ds, gs, d_g):
        cs = c_ref.at[0, 2:6]
        clear_rims(us, hs, ds, gs)
        expand(w1t, k1, True)
        o_two[...] = jnp.zeros(o_two.shape, F32)
        o_out[...] = go[...]
        o_one[...] = jnp.zeros(o_one.shape, F32)
        o_in[...] = jnp.zeros(o_in.shape, F32)

        def entry(c):
            at = pl.ds(c, SPAN)
            for k in range(2):
                put(us, k, c, ut[k, at, :])
                put(us, 8 + k, c, ub[k, at, :])
                put(gs, 2 + k, c, dgm[k, at, :])
            for k in range(6):
                put(us, 2 + k, c, um[k, at, :])
            for r in range(8):
                put(ds, r, c, pick(dht, dhm, dhb, r, at))
                put(hs, r, c, pick(ht, hm, hb, r, at))

        def first(c):
            at = pl.ds(c, SPAN)
            hids = [ref[k, at, :] for ref in (hidt, hidb) for k in range(2)]
            outs = [ref[k, at, :] for ref in (dot_, dob) for k in range(2)]
            for r in (0, 4):
                grads = [pick(dht, dhm, dhb, r + k, at) for k in range(4)]
                groups = windows([near(us, r + j, c) for j in range(6)])
                o_two[...] += kernel_grad(grads, groups)
            o_out[...] += dot_t(jnp.concatenate(hids, axis=0), jnp.concatenate(outs, axis=0))
            for r in (1, 5):
                d_u = conv_pair([near(ds, r - 1 + j, c) for j in range(4)], w2t)
                for k in range(2):
                    rate = sl[r + k - 1, at, :].astype(F32)
                    grad = (half(d_u, k) * rate).astype(BF16)
                    d_g[(r // 5) * 2 + k, at, :] = grad
                    put(gs, r + k - 1, c, grad)
            pu_t[at, :] = conv_half([near(ds, 0, c), near(ds, 1, c)], w2t, 1)
            pu_b[at, :] = conv_half([near(ds, 6, c), near(ds, 7, c)], w2t, 0)

        def second(c):
            at = pl.ds(c, SPAN)
            rows = [near(hs, r, c) for r in range(8)]
            inner = [d_g[0, at, :], d_g[1, at, :], dgm[0, at, :], dgm[1, at, :]]
            inner += [d_g[2, at, :], d_g[3, at, :]]
            for r in (0, 3):
                o_one[...] += kernel_grad(inner[r : r + 3], windows(rows[r : r + 5]))
            grads = [near(gs, r, c) for r in range(6)]
            pz_t[at, :] = conv_half(grads[0:2], w1t, 1)
            pz_b[at, :] = conv_half(grads[4:6], w1t, 0)
            zeros, joined = [], []
            for r in (2, 4):
                conv = conv_pair(grads[r - 2 : r + 2], w1t)
                d_zero = add_pair(dhm[r - 2, at, :], dhm[r - 1, at, :], conv)
                for k in range(2):
                    zeros.append(half(d_zero, k))
                    joined.append(
                        jnp.concatenate([am[r + k - 2, at, :], cs[r + k - 2, at, :]], axis=1)
                    )
            o_in[...] += dot_t(jnp.concatenate(zeros, axis=0), jnp.concatenate(joined, axis=0))

        spans(width, entry)
        spans(width, first)
        spans(width, second)

    return call(
        body,
        [
            ((C, 9 * C), F32),
            ((C, C), F32),
            ((C, 9 * C), F32),
            ((C, 2 * C), F32),
            *[((width, 2 * C), F32)] * 4,
            WIDE,
        ],
        [u_top, u_mid, u_bottom, slope, h_top, h_mid, h_bottom, hid_top, hid_bottom,
         do_top, do_bottom, dh_top, dh_mid, dh_bottom, dg_mid, a_mid, coarse,
         g_out, kern_one, w_two_t],
        [padded(10, width), padded(8, width), padded(8, width), padded(6, width),
         pltpu.VMEM((4, width, C), BF16)],
        LIMIT,
        11,
    )


def backward_edge(low, high, dh_top, dh_bottom, parts, slope_top, slope_bottom, h_low, h_high,
                  h_top, h_bottom, a_top, a_bottom, coarse, g_two, g_out, g_one, g_in, scalars,
                  place, w_one_t, w_two_t):
    width = coarse.shape[2]

    def body(lo, hi, dht, dhb, pu_t, pu_b, pz_t, pz_b, sl_t, sl_b, hlo, hhi, ht, hb, a_t, a_b, c_ref,
             g2, go, g1, gi, sc, place_ref, w1t, w2t, keep_out, send_out,
             ds, gs, hs, own_g, one, total, flat):
        (cs,) = edge_rows(c_ref)
        clear_rims(ds, gs, hs)
        own = (dht, dhb)
        one[...] = g1[...]
        total[...] = gi[...]

        def entry(c):
            at = pl.ds(c, SPAN)
            for side in range(2):
                keep = sc[6 + side]
                for k in range(2):
                    put(ds, 2 * side + k, c, (lo, hi)[side][k, at, :].astype(F32) * keep)
                    put(hs, 1 + 2 * side + k, c, (ht, hb)[side][k, at, :])
                outer = (hlo, hhi)[side][1 - side, at, :].astype(F32)
                put(hs, 5 * side, c, outer * keep)

        def first(c):
            at = pl.ds(c, SPAN)
            for side in range(2):
                d_u = conv_half([near(ds, 2 * side + j, c) for j in range(2)], w2t, side)
                d_u = d_u + (pu_t, pu_b)[side][at, :]
                for k in range(2):
                    rate = (sl_t, sl_b)[side][k, at, :].astype(F32)
                    grad = (half(d_u, k) * rate).astype(BF16)
                    put(gs, 2 * side + k, c, grad)
                    if k != side:
                        own_g[side, at, :] = grad

        def second(c):
            at = pl.ds(c, SPAN)
            zeros, joined, groups = [], [], []
            for side in range(2):
                groups.append([near(hs, 3 * side + j, c) for j in range(3)])
                conv = conv_half([near(gs, 2 * side + j, c) for j in range(2)], w1t, side)
                conv = conv + (pz_t, pz_b)[side][at, :]
                d_zero = add_pair(own[side][0, at, :], own[side][1, at, :], conv)
                for k in range(2):
                    zeros.append(half(d_zero, k))
                    pair = [(a_t, a_b)[side][k, at, :], cs[side][k, at, :]]
                    joined.append(jnp.concatenate(pair, axis=1))
            one[...] += kernel_grad([own_g[0, at, :], own_g[1, at, :]], groups)
            total[...] += dot_t(jnp.concatenate(zeros, axis=0), jnp.concatenate(joined, axis=0))

        spans(width, entry)
        spans(width, first)
        spans(width, second)
        for k in range(9):
            span = slice(k * C, (k + 1) * C)
            flat[AT_ONE + k * C : AT_ONE + (k + 1) * C, :] = one[:, span].T
            flat[AT_TWO + k * C : AT_TWO + (k + 1) * C, :] = g2[:, span].T
        for k in range(2):
            flat[AT_IN + k * C : AT_IN + (k + 1) * C, :] = total[:, k * C : (k + 1) * C].T
        flat[AT_OUT : AT_OUT + C, :] = go[...]
        flat[AT_OUT + C : FLAT, :] = jnp.zeros((FLAT - AT_OUT - C, C), F32)
        part = FLAT // 2
        keep_out[...] = flat[pl.ds(pl.multiple_of(place_ref[0] * part, part), part), :]
        send_out[...] = flat[pl.ds(pl.multiple_of((1 - place_ref[0]) * part, part), part), :]

    part = ((FLAT // 2, C), F32)
    return call(
        body,
        [part, part],
        [low, high, dh_top, dh_bottom, *parts, slope_top, slope_bottom, h_low, h_high, h_top,
         h_bottom, a_top, a_bottom, coarse, g_two, g_out, g_one, g_in, scalars, place, w_one_t,
         w_two_t],
        [padded(4, width), padded(4, width), padded(6, width), pltpu.VMEM((2, width, C), BF16),
         pltpu.VMEM((C, 9 * C), F32), pltpu.VMEM((C, 2 * C), F32), pltpu.VMEM((FLAT, C), F32)],
        LIMIT,
        6,
    )


CORES = ("core", "core")
STAGES = (("x", "y"), ("y", "z"), ("z", "x"))


def shifted(axes, step):
    pairs = []
    for dp in range(8):
        for segment in range(2):
            for tile in range(8):
                at = {"x": tile % 4, "y": dp % 4, "z": (dp // 4) * 2 + tile // 4, "core": segment}
                axis = axes[segment]
                to = dict(at)
                to[axis] = (at[axis] + step) % (2 if axis == "core" else 4)
                target = ((to["z"] // 2) * 4 + to["y"]) * 16 + to["core"] * 8
                target += (to["z"] % 2) * 4 + to["x"]
                pairs.append(((dp * 2 + segment) * 8 + tile, target))
    return pairs


def send(value, axes, step):
    return lax.ppermute(value, AXES, shifted(axes, step))


def scalar(value):
    return jnp.asarray(value, jnp.int32).reshape(1)


def split(terms, parts, index):
    rows = terms[0].shape[0] // parts
    count = len(terms)

    def body(*refs):
        at = refs[0]
        for j in range(parts):
            start = pl.multiple_of(lax.rem(at[0] + j, parts) * rows, 8)
            total = refs[1][pl.ds(start, rows), :]
            for term in refs[2 : 1 + count]:
                total = total + term[pl.ds(start, rows), :]
            refs[1 + count + j][...] = total

    return call(body, [((rows, C), F32)] * parts, [scalar(index), *terms], [], 8)


def join(chunks, index):
    rows = chunks[0].shape[0]
    parts = len(chunks)

    def body(*refs):
        at = refs[0]
        for j in range(parts):
            start = pl.multiple_of(lax.rem(at[0] + j, parts) * rows, 8)
            refs[-1][pl.ds(start, rows), :] = refs[1 + j][...]

    return call(body, [((rows * parts, C), F32)], [scalar(index), *chunks], [], 8)[0]


def add(terms):
    def body(*refs):
        total = refs[0][...]
        for term in refs[1:-1]:
            total = total + term[...]
        refs[-1][...] = total

    return call(body, [(terms[0].shape, F32)], terms, [], 8)[0]


def reduce_all(keep, other, core, first, second):
    one, two, three = STAGES
    got = send(other, CORES, 1)
    own, *rest = split([keep, got], 4, first)
    got = [send(part, one, j + 1) for j, part in enumerate(rest)]
    own, *rest = split([own, *got], 4, second)
    got = [send(part, two, j + 1) for j, part in enumerate(rest)]
    own = add([own, *got])
    own = add([own, *[send(own, three, j + 1) for j in range(3)]])
    own = join([own, *[send(own, two, -(j + 1)) for j in range(3)]], second)
    own = join([own, *[send(own, one, -(j + 1)) for j in range(3)]], first)
    got = send(own, CORES, 1)

    def body(at, a_ref, b_ref, g_in, g_one, g_two, g_out):
        half = FLAT // 2
        first = at[0] == 0

        def rows(start, stop):
            if stop <= half:
                span = slice(start, stop)
            else:
                span = slice(start - half, stop - half)
            low = stop <= half
            return jnp.where(first == low, a_ref[span, :], b_ref[span, :])

        g_in[...] = rows(AT_IN, AT_ONE)
        g_one[...] = rows(AT_ONE, AT_TWO)
        g_two[...] = rows(AT_TWO, AT_OUT)
        g_out[...] = rows(AT_OUT, AT_OUT + C)

    return call(
        body,
        [((2 * C, C), F32), ((9 * C, C), F32), ((9 * C, C), F32), ((C, C), F32)],
        [scalar(core), own, got],
        [],
        8,
    )


def exchange(top, bottom):
    count = lax.axis_size(ROWS)
    down = [(i, (i + 1) % count) for i in range(count)]
    up = [(target, source) for source, target in down]
    return lax.ppermute(bottom, ROWS, down), lax.ppermute(top, ROWS, up)


def on_device(coarse, static_fields, target, noise, sigma, proj_in, kern_one, kern_two, proj_out):
    far = [
        pltpu.with_memory_space_constraint(v, pltpu.HBM)
        for v in (coarse, static_fields, target, noise, proj_in)
    ]
    segment = lax.axis_index("segment")
    tile = lax.axis_index("tile")
    x = tile % 4
    y = lax.axis_index("dp") % 4
    z = lax.axis_index("dp") // 4 * 2 + tile // 4
    row = lax.axis_index(ROWS)
    cells = lax.axis_size("dp") * coarse.shape[1] * lax.axis_size(ROWS) * coarse.shape[2]
    level = sigma[0]
    total_var = level * level + 1.0
    c_in = 1.0 / jnp.sqrt(total_var)
    c_out = level / jnp.sqrt(total_var)
    weight = total_var / (level * level)
    scalars = jnp.stack(
        [
            level,
            c_in,
            1.0 / total_var,
            c_out,
            2.0 * weight * c_out / cells,
            jnp.zeros((), F32),
            (row != 0).astype(F32),
            (row != lax.axis_size(ROWS) - 1).astype(F32),
        ]
    )

    r_top, r_bottom = edge_entry(far[0], far[1], far[4])
    low, high = exchange(r_top, r_bottom)
    u_in, mean_mid, a_mid, h_mid, w_one, w_two = mean_inside(
        r_top, r_bottom, *far[:4], scalars, proj_in, kern_one, kern_two, proj_out,
    )
    mean_top, mean_bottom, a_top, a_bottom, h_top, h_bottom = mean_edge(
        low, high, r_top, r_bottom, u_in, coarse, target, noise, scalars, proj_in, w_one, w_two,
        proj_out,
    )
    h_low, h_high = exchange(h_top, h_bottom)
    (u_mid, slope_mid, dh_mid, dg_mid, *parts, g_out, w_one, w_two,
     w_two_t) = forward_inside(
        h_top, h_mid, h_bottom, mean_mid, target, noise, scalars, kern_one, kern_two, proj_out,
    )
    (u_top, u_bottom, slope_top, slope_bottom, hid_top, hid_bottom, do_top, do_bottom, dh_top,
     dh_bottom) = forward_edge(
        h_low, h_high, h_top, h_bottom, parts, mean_top, mean_bottom, target, noise, scalars,
        w_one, w_two, proj_out,
    )
    dh_low, dh_high = exchange(dh_top, dh_bottom)
    g_two, g_out, g_one, g_in, *parts, w_one_t = backward_inside(
        u_top, u_mid, u_bottom, slope_mid, h_top, h_mid, h_bottom, hid_top, hid_bottom,
        do_top, do_bottom, dh_top, dh_mid, dh_bottom, dg_mid, a_mid, coarse,
        g_out, kern_one, w_two_t,
    )
    keep, other = backward_edge(
        dh_low, dh_high, dh_top, dh_bottom, parts, slope_top, slope_bottom, h_low, h_high,
        h_top, h_bottom, a_top, a_bottom, coarse, g_two, g_out, g_one, g_in, scalars,
        scalar(segment), w_one_t, w_two_t,
    )
    first = jnp.where(segment == 0, x, y)
    second = jnp.where(segment == 0, y, z)
    return tuple(reduce_all(keep, other, segment, first, second))


def solution(mesh):
    placed = (
        P("dp", ("segment", "tile"), None, None),
        P(("segment", "tile"), None, None),
        P("dp", ("segment", "tile"), None, None),
        P("dp", ("segment", "tile"), None, None),
        P("dp"),
        P(),
        P(),
        P(),
        P(),
    )
    return jax.shard_map(
        on_device, mesh=mesh, in_specs=placed, out_specs=(P(), P(), P(), P()), check_vma=False
    )
```
